32 devices in a mesh: dp: 2 (over core), ctx: 8 (over z, x), tp: 2 (over y).
Axes of the slice: x: 2, y: 2, z: 4, core: 2. Of those that a mesh axis runs over, the one named last changes fastest.
Arguments:
- streams: bfloat16 [4, 1024, 3, 8192], P('dp', 'ctx', None, 'tp'), parts along dimension 0, may hold values from -6 to 6
- short_taps: float32 [3, 3, 8192], P(None, None, 'tp'), may hold values from -3.5 to 3.5
- filters: float32 [512, 128], P('tp'), may hold values from -0.5 to 0.5
- queries: bfloat16 [4, 1024, 8192], P('dp', 'ctx', 'tp'), parts along dimension 0, may hold values from -100 to 100
- keys: bfloat16 [4, 1024, 8192], P('dp', 'ctx', 'tp'), parts along dimension 0, may hold values from -10 to 10
- fragment_lengths: int32 [32], P('dp'), parts along dimension 0, may hold values from 1 to 512, 2048 in all
Outputs:
- attended: bfloat16 [4, 1024, 8192], P('dp', 'ctx', 'tp'), parts along dimension 0
The draws below stay inside these ranges and needn't reach their ends.
There are 2 independent parts, one for each index of `dp`. The reference program is written for one: setup_inputs(seed, part) draws one part's arguments, and reference() takes and returns one part's arrays. A program takes and returns all parts, laid end to end along the dimension named above; an argument that names none is the same for every part. Nothing has to cross between parts.
Inputs may be any that keep to these rules, and one draw needn't show every extreme that they name: `fragment_lengths`: the fragments sum to 2048 tokens; the longest has exactly 512.
All inputs are finite; a program needn't handle non-finite values.
Results may differ from the reference program's by a relative error of at most 0.0061.
Values may be sent and summed in bfloat16 or wider, within the bound.
No kernel may reach another device: no remote copies, remote signals or barrier semaphores. Data moves between devices by JAX's collectives and lax.ppermute only.
A program may use at most 192 MiB of HBM per device.

```python
import math
import jax
import jax.numpy as jnp
import numpy as np
from jax import lax

D = 8192
HEADS = 64
HEAD_DIM = 128
GROUP = 16
FILT = 128
ROUNDS = 2
FRAGS = 16
SEQ = 2048


def key_base(key):
    base = jnp.clip(jax.random.normal(jax.random.fold_in(key, 11), (ROUNDS, SEQ // ROUNDS, D), jnp.float32), -5.0, 5.0)
    return base


def draw_keys(key, part):
    return key_base(key).astype(jnp.bfloat16)


def draw_queries(key, part):
    own_key = jax.random.fold_in(key, 3)
    drawn = jnp.clip(jax.random.normal(own_key, (ROUNDS, SEQ // ROUNDS, D), jnp.float32), -5.0, 5.0)
    return drawn.astype(jnp.bfloat16)


def shard_levels(key, shape, pieces, least, high):
    def one(axis_at, parts):
        heights = jax.random.uniform(jax.random.fold_in(jax.random.fold_in(key, 6), axis_at), (parts,), jnp.float32, least / len(pieces), high / len(pieces))
        return jnp.repeat(jnp.exp(heights), shape[axis_at] // parts).reshape((-1,) + (1,) * (len(shape) - axis_at - 1))

    gain = one(*pieces[0])
    for cut in pieces[1:]:
        gain = gain * one(*cut)
    return gain


def split_up(number_of, total, limit, skew):
    portions = [(1 << 20) // math.isqrt(grade ** skew) + 1 for grade in range(2, number_of + 1)]
    surplus, counts = total - limit - (number_of - 1), [1] * (number_of - 1)
    while surplus > 0:
        movable = [i for i in range(number_of - 1) if counts[i] < limit]
        pool, remaining = sum([portions[i] for i in movable]), surplus
        for i in movable:
            addition = min(limit - counts[i], max(1, remaining * portions[i] // pool), surplus)
            counts[i] = counts[i] + addition
            surplus = surplus - addition
    return np.array([limit] + counts)


def ragged(key, count, total, bound, slope):
    if count == 2:
        one = jax.random.randint(key, (), max(1, total - bound), min(bound, total - 1) + 1)
        return jnp.stack([one, total - one])
    lengths = jnp.asarray(split_up(count, total, bound, slope), jnp.int32)
    couples = (count - 1) // 2
    giver, sink = lengths[1:1 + 2 * couples:2], lengths[2:2 + 2 * couples:2]
    slack = jnp.minimum(giver - 1, bound - sink)
    moved = jax.random.randint(jax.random.fold_in(key, 1), (couples,), 0, 1 << 20) % (slack + 1)
    lengths = lengths.at[1:1 + 2 * couples:2].set(giver - moved).at[2:2 + 2 * couples:2].set(sink + moved)
    return lengths[jax.random.permutation(jax.random.fold_in(key, 2), count)]


def bell_draw(stream_key, extent, scale, bound, split=(), held_as=jnp.bfloat16):
    gain = shard_levels(stream_key, extent, split, -0.22, 0.18) if split else 1.0
    entries = jax.random.normal(stream_key, extent, jnp.float32) * scale * gain
    return jnp.minimum(jnp.maximum(entries, -bound), bound).astype(held_as)


def setup_inputs(seed: int = 0, part: int = 0) -> dict:
    seeds = jax.random.split(jax.random.key(seed), 7)
    own_keys = jax.random.split(jax.random.fold_in(seeds[6], part), 7)
    streams = bell_draw(own_keys[0], (ROUNDS, SEQ // ROUNDS, 3, D), 1.0, 6.0, ((1, 8), (3, 2)))
    short_taps = bell_draw(seeds[1], (3, 3, D), 3 ** -0.5, 3.5, ((2, 2),), jnp.float32)
    filters = bell_draw(seeds[2], (D // GROUP, FILT), FILT ** -0.5, 0.5, ((0, 2),), jnp.float32)
    queries = draw_queries(jax.random.fold_in(jax.random.fold_in(seeds[6], part), 71), part)
    keys = draw_keys(jax.random.fold_in(jax.random.fold_in(seeds[6], part), 71), part)
    fragment_lengths = ragged(own_keys[5], FRAGS, SEQ, SEQ // 4, 2).astype(jnp.int32)
    return {"streams": streams, "short_taps": short_taps, "filters": filters, "queries": queries, "keys": keys, "fragment_lengths": fragment_lengths}


def reference(streams, short_taps, filters, queries, keys, fragment_lengths):
    tokens = streams.reshape(SEQ, 3, D).astype(jnp.float32)
    padded = jnp.pad(tokens, ((2, 0), (0, 0), (0, 0)))
    featured = short_taps[:, 0] * padded[2:] + short_taps[:, 1] * padded[1:-1] + short_taps[:, 2] * padded[:-2]
    product = (featured[:, 1] * featured[:, 2]).astype(jnp.bfloat16)
    channel_filters = jnp.repeat(filters, GROUP, axis=0)
    shifted = jnp.pad(product.astype(jnp.float32), ((FILT - 1, 0), (0, 0)))

    def add_tap(tap_index, total):
        window = lax.dynamic_slice_in_dim(shifted, FILT - 1 - tap_index, SEQ, 0)
        return total + channel_filters[:, tap_index] * window

    filtered = lax.fori_loop(0, FILT, add_tap, jnp.zeros((SEQ, D), jnp.float32))
    values = (featured[:, 0] * filtered).astype(jnp.bfloat16)
    positions = jnp.arange(SEQ, dtype=jnp.int32)
    frag_ends = jnp.cumsum(fragment_lengths).astype(jnp.int32)
    fragment = jnp.sum((positions[:, None] >= frag_ends[None, :]).astype(jnp.int32), axis=1)
    visible = (positions[None, :] <= positions[:, None]) & (fragment[None, :] == fragment[:, None])
    query_heads = queries.reshape(SEQ, HEADS, HEAD_DIM).transpose(1, 0, 2)
    key_heads = keys.reshape(SEQ, HEADS, HEAD_DIM).transpose(1, 0, 2)
    value_heads = values.reshape(SEQ, HEADS, HEAD_DIM).transpose(1, 0, 2)
    score_scale = HEAD_DIM ** -0.5

    def one_head(operands):
        query_one, key_one, value_one = operands
        scores = jnp.dot(query_one, key_one.T, preferred_element_type=jnp.float32) * score_scale
        scores = jnp.where(visible, scores, -1e30)
        top = jnp.max(scores, axis=1, keepdims=True)
        raised = jnp.where(visible, jnp.exp(scores - top), 0.0)
        total = jnp.sum(raised, axis=1, keepdims=True)
        weighted = jnp.dot(raised.astype(jnp.bfloat16), value_one, preferred_element_type=jnp.float32)
        return (weighted / total).astype(jnp.bfloat16)

    attended = lax.map(one_head, (query_heads, key_heads, value_heads))
    return attended.transpose(1, 0, 2).reshape(ROUNDS, SEQ // ROUNDS, D)
```

```python
import functools

import jax
import jax.numpy as jnp
from jax import lax
from jax.experimental import pallas as pl
from jax.experimental.pallas import tpu as pltpu
from jax.sharding import PartitionSpec as P

HEAD_DIM = 128
MASKED = -1e30
LOG2E = 1.4426950408889634
VMEM_BYTES = 48 * 1024 * 1024
GROUPS = 2


def params():
    return pltpu.CompilerParams(vmem_limit_bytes=VMEM_BYTES)


def cost(flops, nbytes, exps=0):
    return pl.CostEstimate(flops=flops, bytes_accessed=nbytes, transcendentals=exps)


def feature_kernel(flags, s_ref, halo_ref, taps_ref, p_send, p_own, f_send, f_own):
    step = pl.program_id(0)
    half = pl.num_programs(0) // 2
    rounds, rows = s_ref.shape[1], s_ref.shape[2]
    lanes = s_ref.shape[3]
    row = lax.broadcasted_iota(jnp.int32, (rows, lanes), 0)
    for r in range(rounds):
        featured = []
        for s in range(3):
            now = s_ref[s, r].astype(jnp.float32)
            far = halo_ref[s, r, 0:1].astype(jnp.float32)
            near = halo_ref[s, r, 1:2].astype(jnp.float32)
            one = jnp.where(row == 0, near, pltpu.roll(now, 1, 0))
            two = jnp.where(row == 0, far, jnp.where(row == 1, near, pltpu.roll(now, 2, 0)))
            featured.append(
                taps_ref[s, 0:1] * now + taps_ref[s, 1:2] * one + taps_ref[s, 2:3] * two
            )
        product = (featured[1] * featured[2]).astype(jnp.bfloat16)
        gate = featured[0].astype(jnp.bfloat16)

        @pl.when(step < half)
        def _():
            p_send[r] = product
            f_send[r] = gate

        @pl.when(step >= half)
        def _():
            p_own[r] = product
            f_own[r] = gate


def features(flags, streams, halo, taps):
    _, rounds, rows, channels = streams.shape
    half = channels // 2
    wide = min(512, half)
    steps = half // wide

    def place(j, flags):
        side = jnp.where(j < steps, 1 - flags[0], flags[0])
        return side * steps + j % steps

    out = jax.ShapeDtypeStruct((rounds, rows, half), jnp.bfloat16)
    send = pl.BlockSpec((rounds, rows, wide), lambda j, flags: (0, 0, jnp.minimum(j, steps - 1)))
    own = pl.BlockSpec((rounds, rows, wide), lambda j, flags: (0, 0, jnp.maximum(j - steps, 0)))
    return pl.pallas_call(
        feature_kernel,
        out_shape=(out,) * 4,
        grid_spec=pltpu.PrefetchScalarGridSpec(
            num_scalar_prefetch=1,
            grid=(2 * steps,),
            in_specs=[
                pl.BlockSpec((3, rounds, rows, wide), lambda j, f: (0, 0, 0, place(j, f))),
                pl.BlockSpec((3, rounds, 2, wide), lambda j, f: (0, 0, 0, place(j, f))),
                pl.BlockSpec((3, 3, wide), lambda j, f: (0, 0, place(j, f))),
            ],
            out_specs=(send, own, send, own),
        ),
        compiler_params=params(),
        cost_estimate=cost(20 * streams.size, 4 * streams.size),
        name="features",
    )(flags, streams, halo, taps)


def filter_kernel(flags, p_own, p_recv, h_near, h_wrap, f_own, f_recv, rows_ref, v_ref, tail, gate, toe):
    rounds, block, lanes = p_own.shape
    side, first = flags[0], flags[1]
    mine = pl.multiple_of(side * block, block)
    other = pl.multiple_of((1 - side) * block, block)
    groups = rows_ref.shape[0]
    span = lanes // groups
    for r in range(rounds):
        tail[r, pl.ds(block + mine, block)] = p_own[r]
        tail[r, pl.ds(block + other, block)] = p_recv[r]
        gate[r, pl.ds(mine, block)] = f_own[r]
        gate[r, pl.ds(other, block)] = f_recv[r]

        @pl.when(first == 0)
        def _():
            tail[r, 0:block] = h_near[r]

        @pl.when(first == 1)
        def _():
            if r == 0:
                tail[r, 0:block] = jnp.zeros((block, lanes), jnp.bfloat16)
            else:
                tail[r, 0:block] = h_wrap[r - 1]

    for g in range(groups):
        row = jnp.broadcast_to(rows_ref[g : g + 1], (block, 2 * block))
        toe[g] = pltpu.roll(row, 0, 1, stride=1, stride_axis=0).astype(jnp.bfloat16)
    lane = lax.broadcasted_iota(jnp.int32, (block, 2 * lanes), 1)
    owner = (lane % lanes) // span
    for r in range(rounds):
        right = jnp.concatenate([tail[r, 0 : 2 * block], tail[r, block : 3 * block]], axis=1)
        total = None
        for g in range(groups):
            part = jnp.dot(toe[g], right, preferred_element_type=jnp.float32)
            total = part if g == 0 else jnp.where(owner == g, part, total)
        for b in range(2):
            gated = gate[r, b * block : (b + 1) * block].astype(jnp.float32)
            v_ref[r, b * block : (b + 1) * block] = (
                gated * total[:, b * lanes : (b + 1) * lanes]
            ).astype(jnp.bfloat16)


def filtered_values(flags, p_own, p_recv, h_near, h_wrap, f_own, f_recv, filter_rows):
    rounds, block, channels = p_own.shape
    lanes = 128
    steps = channels // lanes
    groups = filter_rows.shape[0] // steps
    tile = pl.BlockSpec((rounds, block, lanes), lambda j, f: (0, 0, j))
    return pl.pallas_call(
        filter_kernel,
        out_shape=jax.ShapeDtypeStruct((rounds, 2 * block, channels), jnp.bfloat16),
        grid_spec=pltpu.PrefetchScalarGridSpec(
            num_scalar_prefetch=1,
            grid=(steps,),
            in_specs=[
                tile,
                tile,
                tile,
                pl.BlockSpec((rounds - 1, block, lanes), lambda j, f: (0, 0, j)),
                tile,
                tile,
                pl.BlockSpec((groups, 2 * block), lambda j, f: (j, 0)),
            ],
            out_specs=pl.BlockSpec((rounds, 2 * block, lanes), lambda j, f: (0, 0, j)),
            scratch_shapes=[
                pltpu.VMEM((rounds, 3 * block, lanes), jnp.bfloat16),
                pltpu.VMEM((rounds, 2 * block, lanes), jnp.bfloat16),
                pltpu.VMEM((groups, block, 2 * block), jnp.bfloat16),
            ],
        ),
        compiler_params=params(),
        cost_estimate=cost(8 * 4 * block * block * 2 * channels * rounds, 12 * p_own.size),
        name="values",
    )(flags, p_own, p_recv, h_near, h_wrap, f_own, f_recv, filter_rows)


def gather_rows(side, block, out, own, recv):
    mine = pl.multiple_of(side * block, block)
    other = pl.multiple_of((1 - side) * block, block)
    for r in range(own.shape[0]):
        out[r, pl.ds(mine, block)] = own[r]
        out[r, pl.ds(other, block)] = recv[r]


def scores_of(query, key, bias):
    raw = lax.dot_general(query, key, (((1,), (1,)), ((), ())), preferred_element_type=jnp.float32)
    return raw * (HEAD_DIM**-0.5 * LOG2E) + bias


def partial_kernel(
    reach, flags, start_ref, q_own, q_recv, k_own, k_recv, v_ref, o_ref, lse_ref, bias, queries, keys, stat
):
    step = pl.program_id(0)
    rounds, block, lanes = q_own.shape
    size = 2 * block
    heads = lanes // HEAD_DIM

    @pl.when(step == 0)
    def _():
        stat[...] = jnp.zeros_like(stat)
        key_at = lax.broadcasted_iota(jnp.int32, (size, size), 1) - reach * size
        for r in range(rounds):
            start = jnp.concatenate([start_ref[r]] * (size // HEAD_DIM), axis=1)
            bias[r] = jnp.where(key_at >= start, 0.0, MASKED)

    gather_rows(flags[0], block, queries, q_own, q_recv)
    gather_rows(flags[0], block, keys, k_own, k_recv)
    lane = lax.broadcasted_iota(jnp.int32, (size, HEAD_DIM), 1)
    for r in range(rounds):
        for e in range(heads):
            cut = slice(e * HEAD_DIM, (e + 1) * HEAD_DIM)
            scores = scores_of(queries[r, :, cut], keys[r, :, cut], bias[r])
            top = jnp.max(scores, axis=1, keepdims=True)
            raised = jnp.exp2(scores - top)
            total = jnp.sum(raised, axis=1, keepdims=True)
            mixed = jnp.dot(raised.astype(jnp.bfloat16), v_ref[r, :, cut], preferred_element_type=jnp.float32)
            o_ref[r, :, cut] = (mixed / total).astype(jnp.bfloat16)
            stat[r] = jnp.where(lane == step * heads + e, top + jnp.log2(total), stat[r])

    @pl.when(step == pl.num_programs(0) - 1)
    def _():
        for r in range(rounds):
            lse_ref[r] = stat[r].T[0 : lse_ref.shape[1]]


def partial_attention(flags, start, q_own, q_recv, k_own, k_recv, values, reach, first_head, head_count):
    rounds, block, _ = q_own.shape
    size = 2 * block
    per = 2 if head_count % 2 == 0 else 1
    lanes = per * HEAD_DIM
    steps, base = head_count // per, first_head // per
    tile = pl.BlockSpec((rounds, block, lanes), lambda j, f: (0, 0, base + j))
    return pl.pallas_call(
        functools.partial(partial_kernel, reach),
        out_shape=(
            jax.ShapeDtypeStruct((rounds, size, head_count * HEAD_DIM), jnp.bfloat16),
            jax.ShapeDtypeStruct((rounds, head_count, size), jnp.float32),
        ),
        grid_spec=pltpu.PrefetchScalarGridSpec(
            num_scalar_prefetch=1,
            grid=(steps,),
            in_specs=[
                pl.BlockSpec((rounds, size, HEAD_DIM), lambda j, f: (0, 0, 0)),
                tile,
                tile,
                tile,
                tile,
                pl.BlockSpec((rounds, size, lanes), lambda j, f: (0, 0, base + j)),
            ],
            out_specs=(
                pl.BlockSpec((rounds, size, lanes), lambda j, f: (0, 0, j)),
                pl.BlockSpec((rounds, head_count, size), lambda j, f: (0, 0, 0)),
            ),
            scratch_shapes=[
                pltpu.VMEM((rounds, size, size), jnp.float32),
                pltpu.VMEM((rounds, size, lanes), jnp.bfloat16),
                pltpu.VMEM((rounds, size, lanes), jnp.bfloat16),
                pltpu.VMEM((rounds, size, HEAD_DIM), jnp.float32),
            ],
        ),
        compiler_params=params(),
        cost_estimate=cost(
            4 * rounds * size * size * HEAD_DIM * head_count,
            8 * rounds * size * HEAD_DIM * head_count,
            rounds * size * size * head_count,
        ),
        name="partial",
    )(flags, start, q_own, q_recv, k_own, k_recv, values)


def merge_kernel(far_count, flags, start_ref, q_own, q_recv, k_own, k_recv, v_ref, o_near, o_wrap, l_near, l_wrap, *rest):
    far_o = rest[:far_count]
    far_l = rest[far_count : 2 * far_count]
    own_ref, send_ref, bias, queries, keys, stat, spread, result = rest[2 * far_count :]
    step = pl.program_id(0)
    rounds, block, lanes = q_own.shape
    size = 2 * block
    heads = lanes // HEAD_DIM
    side, first = flags[0], flags[1]
    head_count = l_near.shape[1]

    @pl.when(step == 0)
    def _():
        query_at = lax.broadcasted_iota(jnp.int32, (size, size), 0)
        key_at = lax.broadcasted_iota(jnp.int32, (size, size), 1)
        spread[...] = jnp.zeros_like(spread)
        for r in range(rounds):
            start = jnp.concatenate([start_ref[r]] * (size // HEAD_DIM), axis=1)
            bias[r] = jnp.where((key_at >= start) & (key_at <= query_at), 0.0, MASKED)
            wrapped = l_wrap[r - 1] if r else jnp.full((head_count, size), MASKED, jnp.float32)
            spread[0:head_count] = jnp.where(first == 1, wrapped, l_near[r])
            stat[0, r] = spread[...].T
            for n in range(far_count):
                spread[0:head_count] = far_l[n][r]
                stat[n + 1, r] = spread[...].T

    gather_rows(side, block, queries, q_own, q_recv)
    gather_rows(side, block, keys, k_own, k_recv)
    lane = lax.broadcasted_iota(jnp.int32, (size, HEAD_DIM), 1)
    for r in range(rounds):
        for e in range(heads):
            cut = slice(e * HEAD_DIM, (e + 1) * HEAD_DIM)
            scores = scores_of(queries[r, :, cut], keys[r, :, cut], bias[r])
            top = jnp.max(scores, axis=1, keepdims=True)
            raised = jnp.exp2(scores - top)
            total = jnp.sum(raised, axis=1, keepdims=True)
            mixed = jnp.dot(raised.astype(jnp.bfloat16), v_ref[r, :, cut], preferred_element_type=jnp.float32)
            parts, levels = [], []
            for n in range(far_count + 1):
                chosen = jnp.where(lane == step * heads + e, stat[n, r], 0.0)
                levels.append(jnp.sum(chosen, axis=1, keepdims=True))
                if n:
                    parts.append(far_o[n - 1][r, :, cut].astype(jnp.float32))
                else:
                    near = o_near[r, :, cut].astype(jnp.float32)
                    if r:
                        near = jnp.where(first == 1, o_wrap[r - 1, :, cut].astype(jnp.float32), near)
                    parts.append(near)
            high = functools.reduce(jnp.maximum, levels, top)
            share = jnp.exp2(top - high)
            mixed, total = mixed * share, total * share
            for part, level in zip(parts, levels):
                share = jnp.exp2(level - high)
                mixed, total = mixed + part * share, total + share
            result[r, :, cut] = (mixed / total).astype(jnp.bfloat16)
        own_ref[r] = result[r, pl.ds(pl.multiple_of(side * block, block), block)]
        send_ref[r] = result[r, pl.ds(pl.multiple_of((1 - side) * block, block), block)]


def merged_attention(flags, start, q_own, q_recv, k_own, k_recv, values, near, wrap, far, first_head):
    rounds, block, _ = q_own.shape
    size = 2 * block
    o_near, l_near = near
    o_wrap, l_wrap = wrap
    head_count = l_near.shape[1]
    per = 2 if head_count % 2 == 0 else 1
    lanes = per * HEAD_DIM
    steps, base = head_count // per, first_head // per
    tile = pl.BlockSpec((rounds, block, lanes), lambda j, f: (0, 0, base + j))
    wide = pl.BlockSpec((rounds, size, lanes), lambda j, f: (0, 0, base + j))
    out = jax.ShapeDtypeStruct((rounds, block, head_count * HEAD_DIM), jnp.bfloat16)
    out_tile = pl.BlockSpec((rounds, block, lanes), lambda j, f: (0, 0, j))
    group_index = first_head // head_count
    return pl.pallas_call(
        functools.partial(merge_kernel, len(far)),
        out_shape=(out, out),
        grid_spec=pltpu.PrefetchScalarGridSpec(
            num_scalar_prefetch=1,
            grid=(steps,),
            in_specs=[
                pl.BlockSpec((rounds, size, HEAD_DIM), lambda j, f: (0, 0, 0)),
                tile,
                tile,
                tile,
                tile,
                wide,
                pl.BlockSpec((rounds, size, lanes), lambda j, f: (0, 0, j)),
                pl.BlockSpec((rounds - 1, size, lanes), lambda j, f: (0, 0, j)),
                pl.BlockSpec((rounds, head_count, size), lambda j, f: (0, 0, 0)),
                pl.BlockSpec((rounds - 1, head_count, size), lambda j, f: (0, 0, 0)),
            ]
            + [wide] * len(far)
            + [pl.BlockSpec((None, rounds, head_count, size), lambda j, f: (group_index, 0, 0, 0))] * len(far),
            out_specs=(out_tile, out_tile),
            scratch_shapes=[
                pltpu.VMEM((rounds, size, size), jnp.float32),
                pltpu.VMEM((rounds, size, lanes), jnp.bfloat16),
                pltpu.VMEM((rounds, size, lanes), jnp.bfloat16),
                pltpu.VMEM((len(far) + 1, rounds, size, HEAD_DIM), jnp.float32),
                pltpu.VMEM((HEAD_DIM, size), jnp.float32),
                pltpu.VMEM((rounds, size, lanes), jnp.bfloat16),
            ],
        ),
        compiler_params=params(),
        cost_estimate=cost(
            4 * rounds * size * size * HEAD_DIM * head_count,
            12 * rounds * size * HEAD_DIM * head_count,
            rounds * size * size * head_count,
        ),
        name="merged",
    )(
        flags, start, q_own, q_recv, k_own, k_recv, values, o_near, o_wrap, l_near, l_wrap,
        *[o for o, _ in far], *[level for _, level in far],
    )


def body(streams, short_taps, filters, queries, keys, fragment_lengths):
    rounds, block, _, channels = streams.shape
    ctx = lax.axis_size("ctx")
    at = lax.axis_index("ctx")
    side, z = at % 2, at // 2
    depth = ctx // 2
    size = 2 * block
    seq = rounds * ctx * block
    half = channels // 2
    heads = half // HEAD_DIM
    groups = GROUPS if heads % GROUPS == 0 else 1
    per_group = heads // groups
    first, last = z == 0, z == depth - 1
    flags = jnp.stack([side, first.astype(jnp.int32), last.astype(jnp.int32)]).astype(jnp.int32)

    def moved(value, pairs):
        return lax.ppermute(value, "ctx", pairs)

    swap = [(i, i ^ 1) for i in range(ctx)]

    def along(d, chosen=lambda a: True):
        return [(i, i + 2 * d) for i in range(ctx) if 0 <= i + 2 * d < ctx and chosen(i // 2)]

    def around(d):
        if d > 0:
            return [(i, i + 2 * d - ctx) for i in range(ctx) if i + 2 * d >= ctx]
        return [(i, i + 2 * d + ctx) for i in range(ctx) if i + 2 * d < 0]

    def halves(value):
        own = lax.dynamic_slice_in_dim(value, side * half, half, 2)
        send = lax.dynamic_slice_in_dim(value, (1 - side) * half, half, 2)
        return own, send

    ends = jnp.cumsum(fragment_lengths)
    begins = ends - fragment_lengths

    def start_at(positions):
        return jnp.max(jnp.where(begins <= positions[..., None], begins, 0), axis=-1)

    def starts_of(superblocks):
        base = superblocks[:, None] * size
        rel = start_at(base + jnp.arange(size, dtype=jnp.int32)) - base
        return jnp.broadcast_to(rel[:, :, None], rel.shape + (HEAD_DIM,))

    def reaches(superblock, d):
        return start_at(superblock * size) < (superblock - d + 1) * size

    mine = z + jnp.arange(rounds, dtype=jnp.int32) * depth
    own_start = starts_of(mine)
    next_start = starts_of(mine + 1)

    tail = moved(streams[:, block - 2 :], [(i, (i + 1) % ctx) for i in range(ctx)])
    q_own, q_send = halves(queries)
    q_recv = moved(q_send, swap)

    def queries_of_next(value):
        near = moved(value, along(-1))
        wrap = moved(value[1:], around(-1))
        return jnp.concatenate([jnp.where(last, wrap, near[:-1]), near[-1:]], axis=0)

    n_own = queries_of_next(q_own)
    n_recv = queries_of_next(q_recv)

    tail = jnp.where(at == 0, jnp.concatenate([jnp.zeros_like(tail[:1]), tail[:-1]], axis=0), tail)
    p_send, p_own, f_send, f_own = features(
        flags, streams.transpose(2, 0, 1, 3), tail.transpose(2, 0, 1, 3), short_taps
    )
    p_recv = moved(p_send, swap)
    f_recv = moved(f_send, swap)
    k_own, k_send = halves(keys)
    k_recv = moved(k_send, swap)
    rim = jnp.where(side == 1, p_own, p_recv)
    h_near = moved(rim, along(1))
    h_wrap = moved(rim[:-1], around(1))

    own_filters = lax.dynamic_slice_in_dim(filters, side * (filters.shape[0] // 2), filters.shape[0] // 2, 0)
    filter_rows = jnp.pad(own_filters[:, ::-1], ((0, 0), (1, 2 * block - 1 - filters.shape[1])))
    values = filtered_values(flags, p_own, p_recv, h_near, h_wrap, f_own, f_recv, filter_rows)

    far = []
    longest = seq // 4
    far_reach = -(-(longest - 1) // size)
    for d in range(2, far_reach + 1):
        kinds = []
        for r in range(rounds):
            for color in range(2):
                chosen = functools.partial(lambda c, s, a: (a // s) % 2 == c, color, d)
                if along(d, chosen):
                    holds = (z + d < depth) & ((z // d) % 2 == color)
                    asks = (z >= d) & (((z - d) // d) % 2 == color)
                    pairs = along(d, chosen)
                    kinds.append((r, r, holds, asks, pairs, z + d + r * depth, z + r * depth))
        for r in range(rounds - 1):
            holds, asks = z + d >= depth, z < d
            kinds.append((r, r + 1, holds, asks, around(d), z + d + r * depth, z + (r + 1) * depth))
        preds = [
            (holds & reaches(theirs, d)) | (asks & reaches(ours, d))
            for _, _, holds, asks, _, theirs, ours in kinds
        ]
        empty_o = jnp.zeros((rounds, size, half), jnp.bfloat16)
        empty_l = jnp.full((groups, rounds, per_group, size), MASKED, jnp.float32)

        def exchange(kind, k_own, k_recv, values, q_own, q_recv, total_o, total_l):
            key_round, query_round, _, asks, pairs, theirs, _ = kind
            back = [(b, a) for a, b in pairs]
            asked_own = moved(q_own[query_round : query_round + 1], back)
            asked_recv = moved(q_recv[query_round : query_round + 1], back)
            part, level = partial_attention(
                flags, starts_of(theirs[None]), asked_own, asked_recv,
                k_own[key_round : key_round + 1], k_recv[key_round : key_round + 1],
                values[key_round : key_round + 1], d, 0, heads,
            )
            part, level = moved(part, pairs), moved(level, pairs)
            level = level.reshape(groups, per_group, size)
            total_o = total_o.at[query_round].add(part[0])
            total_l = total_l.at[:, query_round].max(jnp.where(asks, level, MASKED))
            return total_o, total_l

        def all_kinds(operands):
            totals = (empty_o, empty_l)
            for kind, pred in zip(kinds, preds):
                totals = lax.cond(
                    pred,
                    lambda *a, kind=kind: exchange(kind, *a),
                    lambda *a: a[-2:],
                    *operands, *totals,
                )
            return totals

        any_pred = functools.reduce(jnp.logical_or, preds)
        far.append(
            lax.cond(
                any_pred, all_kinds, lambda _: (empty_o, empty_l), (k_own, k_recv, values, q_own, q_recv)
            )
        )

    pieces = []
    for g in range(groups):
        part, level = partial_attention(
            flags, next_start, n_own, n_recv, k_own, k_recv, values, 1, g * per_group, per_group
        )
        near = moved(part, along(1)), moved(level, along(1))
        wrap = moved(part[:-1], around(1)), moved(level[:-1], around(1))
        pieces.append((near, wrap))
    mine_out, other_out = [], []
    for g, (near, wrap) in enumerate(pieces):
        own, send = merged_attention(
            flags, own_start, q_own, q_recv, k_own, k_recv, values, near, wrap, far, g * per_group
        )
        mine_out.append(own)
        other_out.append(moved(send, swap))
    mine_out = jnp.concatenate(mine_out, axis=2)
    other_out = jnp.concatenate(other_out, axis=2)
    low = jnp.where(side == 0, mine_out, other_out)
    high = jnp.where(side == 0, other_out, mine_out)
    return jnp.concatenate([low, high], axis=2)


def solution(mesh):
    placed = (
        P("dp", "ctx", None, "tp"),
        P(None, None, "tp"),
        P("tp", None),
        P("dp", "ctx", "tp"),
        P("dp", "ctx", "tp"),
        P("dp"),
    )
    return jax.shard_map(
        body, mesh=mesh, in_specs=placed, out_specs=P("dp", "ctx", "tp"), check_vma=False
    )
```

```python
import functools

import jax
import jax.numpy as jnp
from jax import lax
from jax.experimental import pallas as pl
from jax.experimental.pallas import tpu as pltpu
from jax.sharding import PartitionSpec as P

HEAD_DIM = 128
MASKED = -1e30
LOG2E = 1.4426950408889634
VMEM_BYTES = 48 * 1024 * 1024
GROUPS = 4
VALUE_LANES = 256
ANSWER_GROUPS = 4
STAT_ROWS = 16


def params():
    return pltpu.CompilerParams(vmem_limit_bytes=VMEM_BYTES)


SHORT = pl.CostEstimate(flops=1, bytes_accessed=1, transcendentals=0)


def featured(s_ref, halo_ref, taps_ref, r):
    now = s_ref[r, 0].astype(jnp.float32)
    row = lax.broadcasted_iota(jnp.int32, now.shape, 0)
    far = halo_ref[r, 0, 0:1].astype(jnp.float32)
    near = halo_ref[r, 0, 1:2].astype(jnp.float32)
    one = jnp.where(row == 0, near, pltpu.roll(now, 1, 0))
    two = jnp.where(row == 0, far, jnp.where(row == 1, near, pltpu.roll(now, 2, 0)))
    return taps_ref[0, 0:1] * now + taps_ref[0, 1:2] * one + taps_ref[0, 2:3] * two


def feature_kernel(flags, *refs):
    step = pl.program_id(0)
    half = pl.num_programs(0) // 2
    inputs, (send, own) = refs[:-2], refs[-2:]
    gate = len(inputs) == 4
    for r in range(own.shape[0]):
        value = featured(*inputs[0:3], r)
        if not gate:
            value = value * featured(*inputs[3:6], r)
        value = value.astype(jnp.bfloat16)

        @pl.when(step < half)
        def _():
            if gate:
                send[0, r] = value
                send[1, r] = inputs[3][r]
            else:
                send[r] = value

        @pl.when(step >= half)
        def _():
            own[r] = value


def features(flags, streams, halo, taps, keys, group, groups):
    rounds, _, rows, channels = streams.shape
    part = channels // 2 // groups
    wide = min(512, part)
    steps = part // wide
    chosen = (1, 2) if keys is None else (0,)

    def place(j, flags):
        side = jnp.where(j < steps, 1 - flags[0], flags[0])
        return (side * groups + group) * steps + j % steps

    def sent(j):
        return jnp.minimum(j, steps - 1)

    out = jax.ShapeDtypeStruct((rounds, rows, part), jnp.bfloat16)
    send = pl.BlockSpec((rounds, rows, wide), lambda j, f: (0, 0, sent(j)))
    own = pl.BlockSpec((rounds, rows, wide), lambda j, f: (0, 0, jnp.maximum(j - steps, 0)))
    in_specs = []
    for s in chosen:
        in_specs += [
            pl.BlockSpec((rounds, 1, rows, wide), lambda j, f, s=s: (0, s, 0, place(j, f))),
            pl.BlockSpec((rounds, 1, 2, wide), lambda j, f, s=s: (0, s, 0, place(j, f))),
            pl.BlockSpec((1, 3, wide), lambda j, f, s=s: (s, 0, place(j, f))),
        ]
    operands = (streams, halo, taps) * len(chosen)
    out_shape = out
    if keys is not None:
        in_specs.append(pl.BlockSpec((rounds, rows, wide), lambda j, f: (0, 0, place(sent(j), f))))
        operands += (keys,)
        out_shape = jax.ShapeDtypeStruct((2, rounds, rows, part), jnp.bfloat16)
        send = pl.BlockSpec((2, rounds, rows, wide), lambda j, f: (0, 0, 0, sent(j)))
    return pl.pallas_call(
        feature_kernel,
        out_shape=(out_shape, out),
        grid_spec=pltpu.PrefetchScalarGridSpec(
            num_scalar_prefetch=1, grid=(2 * steps,), in_specs=in_specs, out_specs=(send, own)
        ),
        compiler_params=params(),
        cost_estimate=SHORT,
        name="product" if keys is None else "gate",
    )(flags, *operands)


def filter_kernel(flags, p_own, p_recv, rim, f_own, f_recv, rows_ref, v_ref, product, gate):
    rounds, block, lanes = p_own.shape
    size = 2 * block
    side, first = flags[0], flags[1]
    mine = pl.multiple_of(side * block, block)
    other = pl.multiple_of((1 - side) * block, block)
    for r in range(rounds):
        product[r, pl.ds(block + mine, block)] = p_own[r]
        product[r, pl.ds(block + other, block)] = p_recv[r]
        gate[r, pl.ds(mine, block)] = f_own[r]
        gate[r, pl.ds(other, block)] = f_recv[r]
        if r:
            product[r, 0:block] = rim[r - first]
        else:
            product[r, 0:block] = jnp.where(first == 1, 0.0, rim[r].astype(jnp.float32)).astype(jnp.bfloat16)
    span = HEAD_DIM * rows_ref.shape[0] // lanes
    width = HEAD_DIM // span
    for tile in range(lanes // HEAD_DIM):
        cut = slice(tile * HEAD_DIM, (tile + 1) * HEAD_DIM)
        windows, gates = [], []
        for r in range(rounds):
            flat = product[r, :, cut].astype(jnp.float32).T.astype(jnp.bfloat16)
            windows += [flat[:, 0:size], flat[:, block : 3 * block]]
            gates.append(gate[r, :, cut].astype(jnp.float32).T)
        for g in range(span):
            row = jnp.broadcast_to(rows_ref[tile * span + g : tile * span + g + 1], (block, size))
            toeplitz = pltpu.roll(row, 0, 1, stride=1, stride_axis=0).astype(jnp.bfloat16)
            here = slice(g * width, (g + 1) * width)
            stacked = jnp.concatenate([w[here] for w in windows], axis=0)
            mixed = lax.dot_general(
                stacked, toeplitz, (((1,), (1,)), ((), ())), preferred_element_type=jnp.float32
            )
            for r in range(rounds):
                for b in range(2):
                    at = (2 * r + b) * width
                    v_ref[r, tile * HEAD_DIM + g * width : tile * HEAD_DIM + (g + 1) * width, b * block : (b + 1) * block] = (
                        gates[r][here, b * block : (b + 1) * block] * mixed[at : at + width]
                    ).astype(jnp.bfloat16)


def filtered_values(flags, p_own, p_recv, rim, f_own, fk_recv, filter_rows, group, p_base, total_channels):
    rounds, block, channels = f_own.shape
    lanes = min(VALUE_LANES, channels)
    steps = channels // lanes
    span = lanes * filter_rows.shape[0] // total_channels
    p_tile = pl.BlockSpec((rounds, block, lanes), lambda j, f: (0, 0, p_base // lanes + j))
    f_tile = pl.BlockSpec((rounds, block, lanes), lambda j, f: (0, 0, j))
    return pl.pallas_call(
        filter_kernel,
        out_shape=jax.ShapeDtypeStruct((rounds, channels, 2 * block), jnp.bfloat16),
        grid_spec=pltpu.PrefetchScalarGridSpec(
            num_scalar_prefetch=1,
            grid=(steps,),
            in_specs=[
                p_tile,
                p_tile,
                p_tile,
                f_tile,
                pl.BlockSpec((None, rounds, block, lanes), lambda j, f: (0, 0, 0, j)),
                pl.BlockSpec((span, 2 * block), lambda j, f: (group * steps + j, 0)),
            ],
            out_specs=pl.BlockSpec((rounds, lanes, 2 * block), lambda j, f: (0, j, 0)),
            scratch_shapes=[
                pltpu.VMEM((rounds, 3 * block, lanes), jnp.bfloat16),
                pltpu.VMEM((rounds, 2 * block, lanes), jnp.bfloat16),
            ],
        ),
        compiler_params=params(),
        cost_estimate=SHORT,
        name="values",
    )(flags, p_own, p_recv, rim, f_own, fk_recv, filter_rows)


PAIR = 2
FLAGS = 3


def gather_rows(side, block, out, own, recv):
    mine = pl.multiple_of(side * block, block)
    other = pl.multiple_of((1 - side) * block, block)
    for r in range(own.shape[0]):
        out[r, pl.ds(mine, block)] = own[r]
        out[r, pl.ds(other, block)] = recv[r]


def attend(jobs, query, key, value, bias, finish):
    def scores_of(job):
        return lax.dot_general(
            key(*job), query(*job), (((1,), (1,)), ((), ())), preferred_element_type=jnp.float32
        )

    following = scores_of(jobs[0])
    for n, job in enumerate(jobs):
        scores = following * (HEAD_DIM**-0.5 * LOG2E) + bias(*job)
        if n + 1 < len(jobs):
            following = scores_of(jobs[n + 1])
        top = jnp.max(scores, axis=0, keepdims=True)
        raised = jnp.exp2(scores - top)
        total = jnp.sum(raised, axis=0, keepdims=True)
        mixed = jnp.dot(value(*job), raised.astype(jnp.bfloat16), preferred_element_type=jnp.float32)
        finish(job, mixed, top, total)


def job_list(rounds, lanes, size):
    return [
        (r, slice(c, c + HEAD_DIM), slice(q, q + HEAD_DIM))
        for r in rounds
        for c in range(0, lanes, HEAD_DIM)
        for q in range(0, size, HEAD_DIM)
    ]


def stat_rows(levels):
    row = lax.broadcasted_iota(jnp.int32, (STAT_ROWS, levels[0].shape[1]), 0)
    table = jnp.zeros(row.shape, jnp.float32)
    for e, level in enumerate(levels):
        high = level.astype(jnp.bfloat16).astype(jnp.float32)
        rest = level - high
        middle = rest.astype(jnp.bfloat16).astype(jnp.float32)
        for k, piece in enumerate((high, middle, rest - middle)):
            table = jnp.where(row == 3 * e + k, piece, table)
    return table.astype(jnp.bfloat16)


def partial_kernel(kinds, flags, start_ref, far_start, q_own, q_recv, k_own, k_recv, v_ref, *rest):
    asked = rest[: 2 * len(kinds)]
    o_ref = rest[2 * len(kinds)]
    far_o = rest[2 * len(kinds) + 1 : 3 * len(kinds) + 1]
    bias, queries, keys, far_queries = rest[3 * len(kinds) + 1 :]
    rounds, block, lanes = q_own.shape
    size = 2 * block
    last = flags[2]
    key_at = lax.broadcasted_iota(jnp.int32, (size, size), 0)
    for r in range(rounds):
        seen = key_at - size >= start_ref[r]
        if r == 0:
            seen = seen & (last == 0)
        bias[r] = jnp.where(seen, 0.0, MASKED)
    gather_rows(flags[0], block, queries, q_own, q_recv)
    gather_rows(flags[0], block, keys, k_own, k_recv)

    def written(write):
        levels = {}

        def finish(job, mixed, top, total):
            r, cut, span = job
            write(r, cut, span, (mixed * (1.0 / total)).astype(jnp.bfloat16))
            levels[(r, span.start, cut.start)] = top + jnp.log2(total)
            if cut.stop == lanes:
                rows = stat_rows([levels[(r, span.start, c)] for c in range(0, lanes, HEAD_DIM)])
                write(r, slice(lanes, lanes + STAT_ROWS), span, rows)

        return finish

    def put(r, cut, span, value):
        o_ref[r, cut, span] = value

    def source(r):
        return r - last if r else 0

    attend(
        job_list(range(rounds), lanes, size),
        lambda r, cut, span: queries[r, span, cut],
        lambda r, cut, span: keys[source(r), :, cut],
        lambda r, cut, span: v_ref[source(r), cut],
        lambda r, cut, span: bias[r, :, span],
        written(put),
    )
    for n, (reach, key_round, _) in enumerate(kinds):

        @pl.when(flags[FLAGS + n] == 1)
        def _(n=n, reach=reach, key_round=key_round):
            far_queries[pl.ds(pl.multiple_of(flags[0] * block, block), block)] = asked[2 * n][...]
            far_queries[pl.ds(pl.multiple_of((1 - flags[0]) * block, block), block)] = asked[2 * n + 1][...]

            def put(r, cut, span, value):
                far_o[n][cut, span] = value

            attend(
                job_list([key_round], lanes, size),
                lambda r, cut, span: far_queries[span, cut],
                lambda r, cut, span: keys[r, :, cut],
                lambda r, cut, span: v_ref[r, cut],
                lambda r, cut, span: jnp.where(
                    key_at[:, span] - reach * size >= far_start[n, :, span], 0.0, MASKED
                ),
                written(put),
            )


def own_half(group, groups, rounds, block, lanes):
    return pl.BlockSpec((rounds, block, lanes), lambda j, f: (0, 0, f[0] * groups + group))


def partial_attention(flags, start, far_start, q_own, q_recv, keys, fk_recv, values, asked, kinds, group, groups):
    rounds, block, _ = q_own.shape
    size = 2 * block
    lanes = values.shape[1]
    tile = pl.BlockSpec((rounds, block, lanes), lambda j, f: (0, 0, group))
    rows = lanes + STAT_ROWS
    out = pl.BlockSpec((rows, size), lambda j, f: (0, 0))
    return pl.pallas_call(
        functools.partial(partial_kernel, kinds),
        out_shape=[jax.ShapeDtypeStruct((rounds, rows, size), jnp.bfloat16)]
        + [jax.ShapeDtypeStruct((rows, size), jnp.bfloat16)] * len(kinds),
        grid_spec=pltpu.PrefetchScalarGridSpec(
            num_scalar_prefetch=1,
            grid=(1,),
            in_specs=[
                pl.BlockSpec((rounds, 1, size), lambda j, f: (0, 0, 0)),
                pl.BlockSpec(far_start.shape, lambda j, f: (0, 0, 0)),
                tile,
                tile,
                own_half(group, groups, rounds, block, lanes),
                pl.BlockSpec((None, rounds, block, lanes), lambda j, f: (1, 0, 0, 0)),
                pl.BlockSpec((rounds, lanes, size), lambda j, f: (0, 0, 0)),
            ]
            + [pl.BlockSpec((block, lanes), lambda j, f: (0, group))] * (2 * len(kinds)),
            out_specs=[pl.BlockSpec((rounds, rows, size), lambda j, f: (0, 0, 0))] + [out] * len(kinds),
            scratch_shapes=[
                pltpu.VMEM((rounds, size, size), jnp.float32),
                pltpu.VMEM((rounds, size, lanes), jnp.bfloat16),
                pltpu.VMEM((rounds, size, lanes), jnp.bfloat16),
                pltpu.VMEM((size, lanes), jnp.bfloat16),
            ],
        ),
        compiler_params=params(),
        cost_estimate=SHORT,
        name="partial",
    )(flags, start, far_start, q_own, q_recv, keys, fk_recv, values, *asked)


def merge_kernel(kinds, flags, start_ref, q_own, q_recv, k_own, k_recv, v_ref, near, *rest):
    far = rest[: len(kinds)]
    own_ref, send_ref, bias, queries, keys, result = rest[len(kinds) :]
    rounds, block, lanes = q_own.shape
    size = 2 * block
    side = flags[0]
    key_at = lax.broadcasted_iota(jnp.int32, (size, size), 0)
    query_at = lax.broadcasted_iota(jnp.int32, (size, size), 1)
    for r in range(rounds):
        bias[r] = jnp.where((key_at >= start_ref[r]) & (key_at <= query_at), 0.0, MASKED)
    gather_rows(side, block, queries, q_own, q_recv)
    gather_rows(side, block, keys, k_own, k_recv)

    def finish(job, mixed, top, total):
        r, cut, span = job
        first = 3 * (cut.start // HEAD_DIM)
        parts, levels = [], []
        for n in range(len(kinds) + 1):
            if n and kinds[n - 1][2] != r:
                continue
            block_of = near[r] if n == 0 else far[n - 1]
            rows = block_of[lanes : lanes + STAT_ROWS, span].astype(jnp.float32)
            level = rows[first : first + 1] + rows[first + 1 : first + 2] + rows[first + 2 : first + 3]
            if n:
                level = jnp.where(flags[FLAGS + len(kinds) + n - 1] == 1, level, MASKED)
            parts.append(block_of[cut, span].astype(jnp.float32))
            levels.append(level)
        high = functools.reduce(jnp.maximum, levels, top)
        share = jnp.exp2(top - high)
        mixed, total = mixed * share, total * share
        for part, level in zip(parts, levels):
            share = jnp.exp2(level - high)
            mixed, total = mixed + part * share, total + share
        result[r, span, cut] = (mixed * (1.0 / total)).T.astype(jnp.bfloat16)

    attend(
        job_list(range(rounds), lanes, size),
        lambda r, cut, span: queries[r, span, cut],
        lambda r, cut, span: keys[r, :, cut],
        lambda r, cut, span: v_ref[r, cut],
        lambda r, cut, span: bias[r, :, span],
        finish,
    )
    for r in range(rounds):
        own_ref[r] = result[r, pl.ds(pl.multiple_of(side * block, block), block)]
        send_ref[r] = result[r, pl.ds(pl.multiple_of((1 - side) * block, block), block)]


def merged_attention(flags, start, queries, q_recv, keys, fk_recv, values, near, far, kinds, group, groups):
    rounds, block, _ = q_recv.shape
    size = 2 * block
    lanes = values.shape[1]
    rows = lanes + STAT_ROWS
    own = own_half(group, groups, rounds, block, lanes)
    tile = pl.BlockSpec((rounds, block, lanes), lambda j, f: (0, 0, 0))
    out = jax.ShapeDtypeStruct((rounds, block, lanes), jnp.bfloat16)
    return pl.pallas_call(
        functools.partial(merge_kernel, kinds),
        out_shape=(out, out),
        grid_spec=pltpu.PrefetchScalarGridSpec(
            num_scalar_prefetch=1,
            grid=(1,),
            in_specs=[
                pl.BlockSpec((rounds, 1, size), lambda j, f: (0, 0, 0)),
                own,
                pl.BlockSpec((rounds, block, lanes), lambda j, f: (0, 0, group)),
                own,
                pl.BlockSpec((None, rounds, block, lanes), lambda j, f: (1, 0, 0, 0)),
                pl.BlockSpec((rounds, lanes, size), lambda j, f: (0, 0, 0)),
                pl.BlockSpec((rounds, rows, size), lambda j, f: (0, 0, 0)),
            ]
            + [pl.BlockSpec((rows, size), lambda j, f: (0, 0))] * len(kinds),
            out_specs=(tile, tile),
            scratch_shapes=[
                pltpu.VMEM((rounds, size, size), jnp.float32),
                pltpu.VMEM((rounds, size, lanes), jnp.bfloat16),
                pltpu.VMEM((rounds, size, lanes), jnp.bfloat16),
                pltpu.VMEM((rounds, size, lanes), jnp.bfloat16),
            ],
        ),
        compiler_params=params(),
        cost_estimate=SHORT,
        name="merged",
    )(flags, start, queries, q_recv, keys, fk_recv, values, near, *far)


def after(value, *others):
    return lax.optimization_barrier((value,) + others)[0]


def body(streams, short_taps, filters, queries, keys, fragment_lengths):
    rounds, block, _, channels = streams.shape
    ctx = lax.axis_size("ctx")
    at = lax.axis_index("ctx")
    side, z = at % 2, at // 2
    depth = ctx // 2
    size = 2 * block
    seq = rounds * ctx * block
    half = channels // 2
    groups = min(GROUPS, half // (PAIR * HEAD_DIM))
    part = half // groups
    halves = min(2, groups)
    per_half = groups // halves

    def moved(value, pairs):
        return lax.ppermute(value, "ctx", pairs)

    swap = [(i, i ^ 1) for i in range(ctx)]

    def ring(d):
        return [(i, (i + 2 * d) % ctx) for i in range(ctx)]

    def along(d, chosen):
        return [(i, i + 2 * d) for i in range(ctx) if i + 2 * d < ctx and chosen(i // 2)]

    def around(d):
        return [(i, i + 2 * d - ctx) for i in range(ctx) if i + 2 * d >= ctx]

    ends = jnp.cumsum(fragment_lengths)
    begins = ends - fragment_lengths

    def start_at(positions):
        return jnp.max(jnp.where(begins <= positions[..., None], begins, 0), axis=-1)

    def starts_of(superblocks):
        base = superblocks[:, None] * size
        return (start_at(base + jnp.arange(size, dtype=jnp.int32)) - base)[:, None, :]

    def reaches(superblock, d):
        return start_at(superblock * size) < (superblock - d + 1) * size

    far_reach = -(-(seq // 4 - 1) // size)
    kinds, far_pairs, hold, ask, far_starts = [], [], [], [], []
    for d in range(2, far_reach + 1):
        for r in range(rounds):
            for color in range(2):
                pairs = along(d, functools.partial(lambda c, s, a: (a // s) % 2 == c, color, d))
                if pairs:
                    kinds.append((d, r, r))
                    far_pairs.append(pairs)
                    theirs, ours = z + d + r * depth, z + r * depth
                    hold.append((z + d < depth) & ((z // d) % 2 == color) & reaches(theirs, d))
                    ask.append((z >= d) & (((z - d) // d) % 2 == color) & reaches(ours, d))
                    far_starts.append(theirs)
        for r in range(rounds - 1):
            kinds.append((d, r, r + 1))
            far_pairs.append(around(d))
            theirs, ours = z + d + r * depth, z + (r + 1) * depth
            hold.append((z + d >= depth) & reaches(theirs, d))
            ask.append((z < d) & reaches(ours, d))
            far_starts.append(theirs)
    preds = [a | b for a, b in zip(hold, ask)]
    any_far = functools.reduce(jnp.logical_or, preds)
    flags = jnp.stack([side, z == 0, z == depth - 1] + hold + ask).astype(jnp.int32)
    mine = z + jnp.arange(rounds, dtype=jnp.int32) * depth
    own_start = starts_of(mine)
    next_start = starts_of(jnp.where(z == depth - 1, jnp.roll(mine + 1, 1), mine + 1))
    far_start = starts_of(jnp.stack(far_starts))

    tail = streams[:, block - 2 :].transpose(0, 2, 1, 3)
    queries = after(queries, tail)
    tail = moved(tail, [(i, (i + 1) % ctx) for i in range(ctx)])
    q_send = lax.dynamic_slice_in_dim(queries, (1 - side) * half, half, 2)
    q_recv = moved(q_send, swap)
    q_own = lax.dynamic_slice_in_dim(after(queries, q_send), side * half, half, 2)
    n_own = moved(q_own, ring(-1))

    tail = jnp.where(at == 0, jnp.concatenate([jnp.zeros_like(tail[:1]), tail[:-1]], axis=0), tail)
    first_layout = streams.transpose(0, 2, 1, 3)
    order = flags
    products, p_recv, gates, fk_recv = [], [], [], []
    for h in range(halves):
        products.append(features(order, first_layout, tail, short_taps, None, h, halves))
        order = after(order, products[h][0])
        p_recv.append(moved(products[h][0], swap))

    def chosen_kinds(function, empties, *operands):
        def each(operands):
            return [
                lax.cond(pred, functools.partial(function, n), lambda _: empties, operands)
                for n, pred in enumerate(preds)
            ]

        return lax.cond(any_far, each, lambda _: [empties] * len(kinds), operands)

    def fetch(n, operands):
        back = [(b, a) for a, b in far_pairs[n]]
        return [moved(value[kinds[n][2]], back) for value in operands]

    empty = jnp.zeros((block, half), jnp.bfloat16)
    asked = chosen_kinds(fetch, [empty, empty], after(q_own, order), q_recv)
    order = after(order, asked)
    n_recv = moved(after(q_recv, order), ring(-1))
    asked = [value for pair in asked for value in pair]

    for g in range(groups):
        gates.append(features(order, first_layout, tail, short_taps, keys, g, groups))
        order = after(order, gates[g][0])
        fk_recv.append(moved(gates[g][0], swap))
    rims = [moved(jnp.where(side == 1, products[h][1], p_recv[h]), ring(1)) for h in range(halves)]

    own_filters = lax.dynamic_slice_in_dim(filters, side * (filters.shape[0] // 2), filters.shape[0] // 2, 0)
    filter_rows = jnp.pad(own_filters[:, ::-1], ((0, 0), (1, 2 * block - 1 - filters.shape[1])))
    out = jnp.zeros((rounds, block, channels), jnp.bfloat16)
    nothing = jnp.zeros((part + STAT_ROWS, size), jnp.bfloat16)
    values, near, far = [], [], []

    def merge(g, order, out):
        own, send = merged_attention(
            order, own_start, queries, q_recv, keys, fk_recv[g], values[g], near[g], far[g], kinds, g, groups
        )
        got = moved(send, swap)
        out = lax.dynamic_update_slice_in_dim(out, own, side * half + g * part, 2)
        out = lax.dynamic_update_slice_in_dim(out, got, (1 - side) * half + g * part, 2)
        return send, out

    def answer(n, operands):
        return [moved(piece[n], far_pairs[n]) for piece in operands]

    pending = []
    for g in range(groups):
        values.append(
            filtered_values(
                order, products[g // per_half][1], p_recv[g // per_half], rims[g // per_half], gates[g][1],
                fk_recv[g], filter_rows, g, (g % per_half) * part, half,
            )
        )
        piece, *far_piece = partial_attention(
            order, next_start, far_start, n_own, n_recv, keys, fk_recv[g], values[g], asked, kinds, g, groups
        )
        order = after(order, piece)
        near.append(moved(piece, ring(1)))
        pending.append(far_piece)
        if (g + 1) % ANSWER_GROUPS == 0 or g == groups - 1:
            found = chosen_kinds(answer, [nothing] * len(pending), *after(pending, order))
            order = after(order, found)
            for m in range(len(pending)):
                far.append([one[m] for one in found])
            pending = []
    for g in range(groups):
        _, out = merge(g, order, out)
    return out


def solution(mesh):
    placed = (
        P("dp", "ctx", None, "tp"),
        P(None, None, "tp"),
        P("tp", None),
        P("dp", "ctx", "tp"),
        P("dp", "ctx", "tp"),
        P("dp"),
    )
    return jax.shard_map(
        body, mesh=mesh, in_specs=placed, out_specs=P("dp", "ctx", "tp"), check_vma=False
    )
```

```python
import functools

import jax
import jax.numpy as jnp
from jax import lax
from jax.experimental import pallas as pl
from jax.experimental.pallas import tpu as pltpu
from jax.sharding import PartitionSpec as P

HEAD_DIM = 128
MASKED = -1e30
LOG2E = 1.4426950408889634
VMEM_BYTES = 48 * 1024 * 1024
GROUPS = 4
VALUE_LANES = 256
STAT_ROWS = 16


def params():
    return pltpu.CompilerParams(vmem_limit_bytes=VMEM_BYTES)


SHORT = pl.CostEstimate(flops=1, bytes_accessed=1, transcendentals=0)


def featured(s_ref, halo_ref, taps_ref, r):
    now = s_ref[r, 0].astype(jnp.float32)
    row = lax.broadcasted_iota(jnp.int32, now.shape, 0)
    far = halo_ref[r, 0, 0:1].astype(jnp.float32)
    near = halo_ref[r, 0, 1:2].astype(jnp.float32)
    one = jnp.where(row == 0, near, pltpu.roll(now, 1, 0))
    two = jnp.where(row == 0, far, jnp.where(row == 1, near, pltpu.roll(now, 2, 0)))
    return taps_ref[0, 0:1] * now + taps_ref[0, 1:2] * one + taps_ref[0, 2:3] * two


def feature_kernel(flags, *refs):
    step = pl.program_id(0)
    half = pl.num_programs(0) // 2
    inputs, (send, own) = refs[:-2], refs[-2:]
    gate = len(inputs) == 4
    for r in range(own.shape[0]):
        value = featured(*inputs[0:3], r)
        if not gate:
            value = value * featured(*inputs[3:6], r)
        value = value.astype(jnp.bfloat16)

        @pl.when(step < half)
        def _():
            if gate:
                send[0, r] = value
                send[1, r] = inputs[3][r]
            else:
                send[r] = value

        @pl.when(step >= half)
        def _():
            own[r] = value


def features(flags, streams, halo, taps, keys, group, groups):
    rounds, _, rows, channels = streams.shape
    part = channels // 2 // groups
    wide = min(512, part)
    steps = part // wide
    chosen = (1, 2) if keys is None else (0,)

    def place(j, flags):
        side = jnp.where(j < steps, 1 - flags[0], flags[0])
        return (side * groups + group) * steps + j % steps

    def sent(j):
        return jnp.minimum(j, steps - 1)

    out = jax.ShapeDtypeStruct((rounds, rows, part), jnp.bfloat16)
    send = pl.BlockSpec((rounds, rows, wide), lambda j, f: (0, 0, sent(j)))
    own = pl.BlockSpec((rounds, rows, wide), lambda j, f: (0, 0, jnp.maximum(j - steps, 0)))
    in_specs = []
    for s in chosen:
        in_specs += [
            pl.BlockSpec((rounds, 1, rows, wide), lambda j, f, s=s: (0, s, 0, place(j, f))),
            pl.BlockSpec((rounds, 1, 2, wide), lambda j, f, s=s: (0, s, 0, place(j, f))),
            pl.BlockSpec((1, 3, wide), lambda j, f, s=s: (s, 0, place(j, f))),
        ]
    operands = (streams, halo, taps) * len(chosen)
    out_shape = out
    if keys is not None:
        in_specs.append(pl.BlockSpec((rounds, rows, wide), lambda j, f: (0, 0, place(sent(j), f))))
        operands += (keys,)
        out_shape = jax.ShapeDtypeStruct((2, rounds, rows, part), jnp.bfloat16)
        send = pl.BlockSpec((2, rounds, rows, wide), lambda j, f: (0, 0, 0, sent(j)))
    return pl.pallas_call(
        feature_kernel,
        out_shape=(out_shape, out),
        grid_spec=pltpu.PrefetchScalarGridSpec(
            num_scalar_prefetch=1, grid=(2 * steps,), in_specs=in_specs, out_specs=(send, own)
        ),
        compiler_params=params(),
        cost_estimate=SHORT,
        name="product" if keys is None else "gate",
    )(flags, *operands)


def filter_kernel(flags, p_own, p_recv, rim, wrapped, f_own, f_recv, rows_ref, v_ref, product, gate):
    rounds, block, lanes = p_own.shape
    size = 2 * block
    side, first = flags[0], flags[1]
    mine = pl.multiple_of(side * block, block)
    other = pl.multiple_of((1 - side) * block, block)
    for r in range(rounds):
        product[r, pl.ds(block + mine, block)] = p_own[r]
        product[r, pl.ds(block + other, block)] = p_recv[r]
        gate[r, pl.ds(mine, block)] = f_own[r]
        gate[r, pl.ds(other, block)] = f_recv[r]

        @pl.when(first == 0)
        def _():
            product[r, 0:block] = rim[r]

        @pl.when(first == 1)
        def _():
            product[r, 0:block] = wrapped[r - 1] if r else jnp.zeros((block, lanes), jnp.bfloat16)

    span = HEAD_DIM * rows_ref.shape[0] // lanes
    width = HEAD_DIM // span
    for tile in range(lanes // HEAD_DIM):
        cut = slice(tile * HEAD_DIM, (tile + 1) * HEAD_DIM)
        windows, gates = [], []
        for r in range(rounds):
            flat = product[r, :, cut].astype(jnp.float32).T.astype(jnp.bfloat16)
            windows += [flat[:, 0:size], flat[:, block : 3 * block]]
            gates.append(gate[r, :, cut].astype(jnp.float32).T)
        for g in range(span):
            row = jnp.broadcast_to(rows_ref[tile * span + g : tile * span + g + 1], (block, size))
            toeplitz = pltpu.roll(row, 0, 1, stride=1, stride_axis=0).astype(jnp.bfloat16)
            here = slice(g * width, (g + 1) * width)
            stacked = jnp.concatenate([w[here] for w in windows], axis=0)
            mixed = lax.dot_general(
                stacked, toeplitz, (((1,), (1,)), ((), ())), preferred_element_type=jnp.float32
            )
            for r in range(rounds):
                for b in range(2):
                    at = (2 * r + b) * width
                    v_ref[r, tile * HEAD_DIM + g * width : tile * HEAD_DIM + (g + 1) * width, b * block : (b + 1) * block] = (
                        gates[r][here, b * block : (b + 1) * block] * mixed[at : at + width]
                    ).astype(jnp.bfloat16)


def filtered_values(
    flags, p_own, p_recv, rim, wrapped, f_own, fk_recv, filter_rows, group, within, channels, total_channels
):
    rounds, block, _ = f_own.shape
    lanes = min(VALUE_LANES, channels)
    steps = channels // lanes
    span = lanes * filter_rows.shape[0] // total_channels
    p_tile = pl.BlockSpec((rounds, block, lanes), lambda j, f: (0, 0, group * steps + j))
    tile = pl.BlockSpec((rounds, block, lanes), lambda j, f: (0, 0, within * steps + j))
    return pl.pallas_call(
        filter_kernel,
        out_shape=jax.ShapeDtypeStruct((rounds, channels, 2 * block), jnp.bfloat16),
        grid_spec=pltpu.PrefetchScalarGridSpec(
            num_scalar_prefetch=1,
            grid=(steps,),
            in_specs=[
                p_tile,
                p_tile,
                p_tile,
                pl.BlockSpec((rounds - 1, block, lanes), lambda j, f: (0, 0, group * steps + j)),
                tile,
                pl.BlockSpec((None, rounds, block, lanes), lambda j, f: (0, 0, 0, within * steps + j)),
                pl.BlockSpec((span, 2 * block), lambda j, f: (group * steps + j, 0)),
            ],
            out_specs=pl.BlockSpec((rounds, lanes, 2 * block), lambda j, f: (0, j, 0)),
            scratch_shapes=[
                pltpu.VMEM((rounds, 3 * block, lanes), jnp.bfloat16),
                pltpu.VMEM((rounds, 2 * block, lanes), jnp.bfloat16),
            ],
        ),
        compiler_params=params(),
        cost_estimate=SHORT,
        name="values",
    )(flags, p_own, p_recv, rim, wrapped, f_own, fk_recv, filter_rows)


PAIR = 2
FLAGS = 3


def gather_rows(side, block, out, own, recv):
    mine = pl.multiple_of(side * block, block)
    other = pl.multiple_of((1 - side) * block, block)
    for r in range(own.shape[0]):
        out[r, pl.ds(mine, block)] = own[r]
        out[r, pl.ds(other, block)] = recv[r]


def attend(jobs, query, key, value, bias, finish):
    def scores_of(job):
        return lax.dot_general(
            key(*job), query(*job), (((1,), (1,)), ((), ())), preferred_element_type=jnp.float32
        )

    following = scores_of(jobs[0])
    for n, job in enumerate(jobs):
        scores = following * (HEAD_DIM**-0.5 * LOG2E) + bias(*job)
        if n + 1 < len(jobs):
            following = scores_of(jobs[n + 1])
        top = jnp.max(scores, axis=0, keepdims=True)
        raised = jnp.exp2(scores - top)
        total = jnp.sum(raised, axis=0, keepdims=True)
        mixed = jnp.dot(value(*job), raised.astype(jnp.bfloat16), preferred_element_type=jnp.float32)
        finish(job, mixed, top, total)


def job_list(rounds, lanes, size):
    return [
        (r, slice(c, c + HEAD_DIM), slice(q, q + HEAD_DIM))
        for r in rounds
        for c in range(0, lanes, HEAD_DIM)
        for q in range(0, size, HEAD_DIM)
    ]


def stat_rows(levels):
    row = lax.broadcasted_iota(jnp.int32, (STAT_ROWS, levels[0].shape[1]), 0)
    table = jnp.zeros(row.shape, jnp.float32)
    for e, level in enumerate(levels):
        high = level.astype(jnp.bfloat16).astype(jnp.float32)
        rest = level - high
        middle = rest.astype(jnp.bfloat16).astype(jnp.float32)
        for k, piece in enumerate((high, middle, rest - middle)):
            table = jnp.where(row == 3 * e + k, piece, table)
    return table.astype(jnp.bfloat16)


def partial_kernel(kinds, flags, start_ref, far_start, q_own, q_recv, wrapped, k_own, k_recv, v_ref, *rest):
    asked = rest[: len(kinds)]
    o_ref = rest[len(kinds)]
    far_o = rest[len(kinds) + 1 : 2 * len(kinds) + 1]
    bias, queries, keys, far_queries = rest[2 * len(kinds) + 1 :]
    rounds, block, lanes = q_own.shape
    size = 2 * block
    last = flags[2]
    key_at = lax.broadcasted_iota(jnp.int32, (size, size), 0)
    for r in range(rounds):
        seen = key_at - size >= start_ref[r]
        if r == 0:
            seen = seen & (last == 0)
        bias[r] = jnp.where(seen, 0.0, MASKED)
    gather_rows(flags[0], block, queries, q_own, q_recv)
    gather_rows(flags[0], block, keys, k_own, k_recv)

    @pl.when(last == 1)
    def _():
        gather_rows(flags[0], block, queries.at[rounds - 1 :], wrapped.at[0:1], wrapped.at[1:2])

    def written(write):
        levels = {}

        def finish(job, mixed, top, total):
            r, cut, span = job
            write(r, cut, span, (mixed * (1.0 / total)).astype(jnp.bfloat16))
            levels[(r, span.start, cut.start)] = top + jnp.log2(total)
            if cut.stop == lanes:
                rows = stat_rows([levels[(r, span.start, c)] for c in range(0, lanes, HEAD_DIM)])
                write(r, slice(lanes, lanes + STAT_ROWS), span, rows)

        return finish

    def put(r, cut, span, value):
        o_ref[r, cut, span] = value

    def source(r):
        return r - last if r else 0

    attend(
        job_list(range(rounds), lanes, size),
        lambda r, cut, span: queries[r, span, cut],
        lambda r, cut, span: keys[source(r), :, cut],
        lambda r, cut, span: v_ref[source(r), cut],
        lambda r, cut, span: bias[r, :, span],
        written(put),
    )
    for n, (reach, key_round, _) in enumerate(kinds):

        @pl.when(flags[FLAGS + n] == 1)
        def _(n=n, reach=reach, key_round=key_round):
            far_queries[pl.ds(pl.multiple_of(flags[0] * block, block), block)] = asked[n][0]
            far_queries[pl.ds(pl.multiple_of((1 - flags[0]) * block, block), block)] = asked[n][1]

            def put(r, cut, span, value):
                far_o[n][cut, span] = value

            attend(
                job_list([key_round], lanes, size),
                lambda r, cut, span: far_queries[span, cut],
                lambda r, cut, span: keys[r, :, cut],
                lambda r, cut, span: v_ref[r, cut],
                lambda r, cut, span: jnp.where(
                    key_at[:, span] - reach * size >= far_start[n, :, span], 0.0, MASKED
                ),
                written(put),
            )


def own_half(group, groups, rounds, block, lanes):
    return pl.BlockSpec((rounds, block, lanes), lambda j, f: (0, 0, f[0] * groups + group))


def partial_attention(
    flags, start, far_start, q_own, q_recv, wrapped, keys, fk_recv, values, asked, kinds, group, groups, within
):
    rounds, block, _ = q_own.shape
    size = 2 * block
    lanes = values.shape[1]
    tile = pl.BlockSpec((rounds, block, lanes), lambda j, f: (0, 0, group))
    rows = lanes + STAT_ROWS
    out = pl.BlockSpec((rows, size), lambda j, f: (0, 0))
    return pl.pallas_call(
        functools.partial(partial_kernel, kinds),
        out_shape=[jax.ShapeDtypeStruct((rounds, rows, size), jnp.bfloat16)]
        + [jax.ShapeDtypeStruct((rows, size), jnp.bfloat16)] * len(kinds),
        grid_spec=pltpu.PrefetchScalarGridSpec(
            num_scalar_prefetch=1,
            grid=(1,),
            in_specs=[
                pl.BlockSpec((rounds, 1, size), lambda j, f: (0, 0, 0)),
                pl.BlockSpec(far_start.shape, lambda j, f: (0, 0, 0)),
                tile,
                tile,
                pl.BlockSpec((2, block, lanes), lambda j, f: (0, 0, group)),
                own_half(group, groups, rounds, block, lanes),
                pl.BlockSpec((None, rounds, block, lanes), lambda j, f: (1, 0, 0, within)),
                pl.BlockSpec((rounds, lanes, size), lambda j, f: (0, 0, 0)),
            ]
            + [pl.BlockSpec((2, block, lanes), lambda j, f: (0, 0, group))] * len(kinds),
            out_specs=[pl.BlockSpec((rounds, rows, size), lambda j, f: (0, 0, 0))] + [out] * len(kinds),
            scratch_shapes=[
                pltpu.VMEM((rounds, size, size), jnp.float32),
                pltpu.VMEM((rounds, size, lanes), jnp.bfloat16),
                pltpu.VMEM((rounds, size, lanes), jnp.bfloat16),
                pltpu.VMEM((size, lanes), jnp.bfloat16),
            ],
        ),
        compiler_params=params(),
        cost_estimate=SHORT,
        name="partial",
    )(flags, start, far_start, q_own, q_recv, wrapped, keys, fk_recv, values, *asked)


def merge_kernel(kinds, flags, start_ref, q_own, q_recv, k_own, k_recv, v_ref, near, *rest):
    far = rest[: len(kinds)]
    own_ref, send_ref, bias, queries, keys, result = rest[len(kinds) :]
    rounds, block, lanes = q_own.shape
    size = 2 * block
    side = flags[0]
    key_at = lax.broadcasted_iota(jnp.int32, (size, size), 0)
    query_at = lax.broadcasted_iota(jnp.int32, (size, size), 1)
    for r in range(rounds):
        bias[r] = jnp.where((key_at >= start_ref[r]) & (key_at <= query_at), 0.0, MASKED)
    gather_rows(side, block, queries, q_own, q_recv)
    gather_rows(side, block, keys, k_own, k_recv)

    def finish(job, mixed, top, total):
        r, cut, span = job
        first = 3 * (cut.start // HEAD_DIM)
        parts, levels = [], []
        for n in range(len(kinds) + 1):
            if n and kinds[n - 1][2] != r:
                continue
            block_of = near[r] if n == 0 else far[n - 1]
            rows = block_of[lanes : lanes + STAT_ROWS, span].astype(jnp.float32)
            level = rows[first : first + 1] + rows[first + 1 : first + 2] + rows[first + 2 : first + 3]
            part = block_of[cut, span].astype(jnp.float32)
            if n:
                asks = flags[FLAGS + len(kinds) + n - 1] == 1
                level, part = jnp.where(asks, level, MASKED), jnp.where(asks, part, 0.0)
            parts.append(part)
            levels.append(level)
        high = functools.reduce(jnp.maximum, levels, top)
        share = jnp.exp2(top - high)
        mixed, total = mixed * share, total * share
        for part, level in zip(parts, levels):
            share = jnp.exp2(level - high)
            mixed, total = mixed + part * share, total + share
        result[r, span, cut] = (mixed * (1.0 / total)).T.astype(jnp.bfloat16)

    attend(
        job_list(range(rounds), lanes, size),
        lambda r, cut, span: queries[r, span, cut],
        lambda r, cut, span: keys[r, :, cut],
        lambda r, cut, span: v_ref[r, cut],
        lambda r, cut, span: bias[r, :, span],
        finish,
    )
    for r in range(rounds):
        own_ref[r] = result[r, pl.ds(pl.multiple_of(side * block, block), block)]
        send_ref[r] = result[r, pl.ds(pl.multiple_of((1 - side) * block, block), block)]


def merged_attention(flags, start, queries, q_recv, keys, fk_recv, values, near, found, place, kinds, group, groups, within):
    rounds, block, _ = q_recv.shape
    size = 2 * block
    lanes = values.shape[1]
    rows = lanes + STAT_ROWS
    own = own_half(group, groups, rounds, block, lanes)
    tile = pl.BlockSpec((rounds, block, lanes), lambda j, f: (0, 0, 0))
    out = jax.ShapeDtypeStruct((rounds, block, lanes), jnp.bfloat16)
    return pl.pallas_call(
        functools.partial(merge_kernel, kinds),
        out_shape=(out, out),
        grid_spec=pltpu.PrefetchScalarGridSpec(
            num_scalar_prefetch=1,
            grid=(1,),
            in_specs=[
                pl.BlockSpec((rounds, 1, size), lambda j, f: (0, 0, 0)),
                own,
                pl.BlockSpec((rounds, block, lanes), lambda j, f: (0, 0, group)),
                own,
                pl.BlockSpec((None, rounds, block, lanes), lambda j, f: (1, 0, 0, within)),
                pl.BlockSpec((rounds, lanes, size), lambda j, f: (0, 0, 0)),
                pl.BlockSpec((rounds, rows, size), lambda j, f: (0, 0, 0)),
            ]
            + [pl.BlockSpec((None, rows, size), lambda j, f: (place, 0, 0))] * len(kinds),
            out_specs=(tile, tile),
            scratch_shapes=[
                pltpu.VMEM((rounds, size, size), jnp.float32),
                pltpu.VMEM((rounds, size, lanes), jnp.bfloat16),
                pltpu.VMEM((rounds, size, lanes), jnp.bfloat16),
                pltpu.VMEM((rounds, size, lanes), jnp.bfloat16),
            ],
        ),
        compiler_params=params(),
        cost_estimate=SHORT,
        name="merged",
    )(flags, start, queries, q_recv, keys, fk_recv, values, near, *found)


def unwritten(shape):
    return pl.pallas_call(
        lambda ref: None,
        out_shape=jax.ShapeDtypeStruct(shape, jnp.bfloat16),
        out_specs=pl.BlockSpec(memory_space=pl.ANY),
        cost_estimate=SHORT,
        name="unwritten",
    )()


def after(value, *others):
    return lax.optimization_barrier((value,) + others)[0]


def body(streams, short_taps, filters, queries, keys, fragment_lengths):
    rounds, block, _, channels = streams.shape
    ctx = lax.axis_size("ctx")
    at = lax.axis_index("ctx")
    side, z = at % 2, at // 2
    depth = ctx // 2
    size = 2 * block
    seq = rounds * ctx * block
    half = channels // 2
    groups = min(GROUPS, half // (PAIR * HEAD_DIM))
    part = half // groups
    halves = min(2, groups)
    per_half = groups // halves

    def moved(value, pairs):
        return lax.ppermute(value, "ctx", pairs)

    swap = [(i, i ^ 1) for i in range(ctx)]

    def ring(d):
        return [(i, (i + 2 * d) % ctx) for i in range(ctx)]

    def along(d, chosen=lambda z: True):
        return [(i, i + 2 * d) for i in range(ctx) if 0 <= i + 2 * d < ctx and chosen(i // 2)]

    def around(d):
        return [(i, (i + 2 * d) % ctx) for i in range(ctx) if not 0 <= i + 2 * d < ctx]

    ends = jnp.cumsum(fragment_lengths)
    begins = ends - fragment_lengths

    def start_at(positions):
        return jnp.max(jnp.where(begins <= positions[..., None], begins, 0), axis=-1)

    def starts_of(superblocks):
        base = superblocks[:, None] * size
        return (start_at(base + jnp.arange(size, dtype=jnp.int32)) - base)[:, None, :]

    def reaches(superblock, d):
        return start_at(superblock * size) < (superblock - d + 1) * size

    far_reach = -(-(seq // 4 - 1) // size)
    kinds, far_pairs, hold, ask, far_starts = [], [], [], [], []
    for d in range(2, far_reach + 1):
        for r in range(rounds):
            for color in range(2):
                pairs = along(d, functools.partial(lambda c, s, a: (a // s) % 2 == c, color, d))
                if pairs:
                    kinds.append((d, r, r))
                    far_pairs.append(pairs)
                    theirs, ours = z + d + r * depth, z + r * depth
                    hold.append((z + d < depth) & ((z // d) % 2 == color) & reaches(theirs, d))
                    ask.append((z >= d) & (((z - d) // d) % 2 == color) & reaches(ours, d))
                    far_starts.append(theirs)
        for r in range(rounds - 1):
            kinds.append((d, r, r + 1))
            far_pairs.append(around(d))
            theirs, ours = z + d + r * depth, z + (r + 1) * depth
            hold.append((z + d >= depth) & reaches(theirs, d))
            ask.append((z < d) & reaches(ours, d))
            far_starts.append(theirs)
    preds = [a | b for a, b in zip(hold, ask)]
    any_far = functools.reduce(jnp.logical_or, preds)
    flags = jnp.stack([side, z == 0, z == depth - 1] + hold + ask).astype(jnp.int32)
    mine = z + jnp.arange(rounds, dtype=jnp.int32) * depth
    own_start = starts_of(mine)
    next_start = starts_of(jnp.where(z == depth - 1, jnp.roll(mine + 1, 1), mine + 1))
    far_start = starts_of(jnp.stack(far_starts))

    tail = streams[:, block - 2 :].transpose(0, 2, 1, 3)
    queries = after(queries, tail)
    tail = moved(tail, [(i, (i + 1) % ctx) for i in range(ctx)])
    q_send = lax.dynamic_slice_in_dim(queries, (1 - side) * half, half, 2)
    q_recv = moved(q_send, swap)
    q_own = lax.dynamic_slice_in_dim(after(queries, q_send), side * half, half, 2)
    n_own = moved(q_own, along(-1))

    tail = jnp.where(at == 0, jnp.concatenate([jnp.zeros_like(tail[:1]), tail[:-1]], axis=0), tail)
    first_layout = streams.transpose(0, 2, 1, 3)
    order = flags
    p_send, p_own = features(order, first_layout, tail, short_taps, None, 0, 1)
    order = after(order, p_send)
    p_recv = moved(p_send, swap)
    q_late = after(q_recv, p_send, n_own)
    n_recv = moved(q_late, along(-1))
    wrapped_send = jnp.stack([q_own[-1], q_late[-1]])
    wrapped = moved(wrapped_send, around(-1))
    gates, fk_recv = [], []
    for h in range(halves):
        if h:
            order = after(order, wrapped_send)
        gates.append(features(order, first_layout, tail, short_taps, keys, h, halves))
        order = after(order, gates[h][0])
        fk_recv.append(moved(gates[h][0], swap))
    rim_send = jnp.where(side == 1, p_own, after(p_recv, order))
    rim = moved(rim_send, along(1))
    rim_wrapped = moved(rim_send[:-1], around(1))

    def chosen_kinds(function, empty, *operands):
        def each(operands):
            return [
                lax.cond(pred, functools.partial(function, n), lambda _: unwritten(empty), operands)
                for n, pred in enumerate(preds)
            ]

        return lax.cond(any_far, each, lambda _: [unwritten(empty) for _ in kinds], operands)

    def fetch(n, operands):
        back = [(b, a) for a, b in far_pairs[n]]
        return moved(jnp.stack([value[kinds[n][2]] for value in operands]), back)

    asked = chosen_kinds(
        fetch, (2, block, half), *after((q_own, q_late), order, n_recv, wrapped, rim_send)
    )
    order = after(order, asked)

    own_filters = lax.dynamic_slice_in_dim(filters, side * (filters.shape[0] // 2), filters.shape[0] // 2, 0)
    filter_rows = jnp.pad(own_filters[:, ::-1], ((0, 0), (1, 2 * block - 1 - filters.shape[1])))
    out = jnp.zeros((rounds, block, channels), jnp.bfloat16)
    values, near = [], []

    def merge(g, order, out):
        own, send = merged_attention(
            order, own_start, queries, q_recv, keys, fk_recv[g // per_half], values[g], near[g], *far[g], kinds, g, groups,
            g % per_half,
        )
        got = moved(send, swap)
        out = lax.dynamic_update_slice_in_dim(out, own, side * half + g * part, 2)
        out = lax.dynamic_update_slice_in_dim(out, got, (1 - side) * half + g * part, 2)
        return send, out

    def answer(n, operands):
        return moved(jnp.stack([piece[n] for piece in operands]), far_pairs[n])

    far_pieces = []
    for g in range(groups):
        h, within = g // per_half, g % per_half
        values.append(
            filtered_values(
                order, p_own, p_recv, rim, rim_wrapped, gates[h][1], fk_recv[h], filter_rows,
                g, within, part, half,
            )
        )
        piece, *far_piece = partial_attention(
            order, next_start, far_start, n_own, n_recv, wrapped, keys, fk_recv[h], values[g], asked,
            kinds, g, groups, within,
        )
        order = after(order, piece)
        far_pieces.append(far_piece)
        if g == groups - 1:
            found = chosen_kinds(answer, (groups, part + STAT_ROWS, size), *after(far_pieces, order))
            order = after(order, found)
            piece = after(piece, found)
        near.append(moved(after(piece, *near[-2:-1]), ring(1)))
    far = [(found, g) for g in range(groups)]
    for g in range(groups):
        _, out = merge(g, order, out)
    return out


def solution(mesh):
    placed = (
        P("dp", "ctx", None, "tp"),
        P(None, None, "tp"),
        P("tp", None),
        P("dp", "ctx", "tp"),
        P("dp", "ctx", "tp"),
        P("dp"),
    )
    return jax.shard_map(
        body, mesh=mesh, in_specs=placed, out_specs=P("dp", "ctx", "tp"), check_vma=False
    )
```

```python
import functools

import jax
import jax.numpy as jnp
from jax import lax
from jax.experimental import pallas as pl
from jax.experimental.pallas import tpu as pltpu
from jax.sharding import PartitionSpec as P

HEAD_DIM = 128
MASKED = -1e30
LOG2E = 1.4426950408889634
VMEM_BYTES = 48 * 1024 * 1024
GROUPS = 4
VALUE_LANES = 256
STAT_ROWS = 16


def params():
    return pltpu.CompilerParams(vmem_limit_bytes=VMEM_BYTES)


SHORT = pl.CostEstimate(flops=1, bytes_accessed=1, transcendentals=0)


def featured(s_ref, halo_ref, taps_ref, r):
    now = s_ref[r, 0].astype(jnp.float32)
    row = lax.broadcasted_iota(jnp.int32, now.shape, 0)
    far = halo_ref[r, 0, 0:1].astype(jnp.float32)
    near = halo_ref[r, 0, 1:2].astype(jnp.float32)
    one = jnp.where(row == 0, near, pltpu.roll(now, 1, 0))
    two = jnp.where(row == 0, far, jnp.where(row == 1, near, pltpu.roll(now, 2, 0)))
    return taps_ref[0, 0:1] * now + taps_ref[0, 1:2] * one + taps_ref[0, 2:3] * two


def feature_kernel(flags, *refs):
    step = pl.program_id(0)
    half = pl.num_programs(0) // 2
    inputs, (send, own) = refs[:-2], refs[-2:]
    gate = len(inputs) == 4
    for r in range(own.shape[0]):
        value = featured(*inputs[0:3], r)
        if not gate:
            value = value * featured(*inputs[3:6], r)
        value = value.astype(jnp.bfloat16)

        @pl.when(step < half)
        def _():
            if gate:
                send[0, r] = value
                send[1, r] = inputs[3][r]
            else:
                send[r] = value

        @pl.when(step >= half)
        def _():
            own[r] = value


def features(flags, streams, halo, taps, keys, group, groups):
    rounds, _, rows, channels = streams.shape
    part = channels // 2 // groups
    wide = min(512, part)
    steps = part // wide
    chosen = (1, 2) if keys is None else (0,)

    def place(j, flags):
        side = jnp.where(j < steps, 1 - flags[0], flags[0])
        return (side * groups + group) * steps + j % steps

    def sent(j):
        return jnp.minimum(j, steps - 1)

    out = jax.ShapeDtypeStruct((rounds, rows, part), jnp.bfloat16)
    send = pl.BlockSpec((rounds, rows, wide), lambda j, f: (0, 0, sent(j)))
    own = pl.BlockSpec((rounds, rows, wide), lambda j, f: (0, 0, jnp.maximum(j - steps, 0)))
    in_specs = []
    for s in chosen:
        in_specs += [
            pl.BlockSpec((rounds, 1, rows, wide), lambda j, f, s=s: (0, s, 0, place(j, f))),
            pl.BlockSpec((rounds, 1, 2, wide), lambda j, f, s=s: (0, s, 0, place(j, f))),
            pl.BlockSpec((1, 3, wide), lambda j, f, s=s: (s, 0, place(j, f))),
        ]
    operands = (streams, halo, taps) * len(chosen)
    out_shape = out
    if keys is not None:
        in_specs.append(pl.BlockSpec((rounds, rows, wide), lambda j, f: (0, 0, place(sent(j), f))))
        operands += (keys,)
        out_shape = jax.ShapeDtypeStruct((2, rounds, rows, part), jnp.bfloat16)
        send = pl.BlockSpec((2, rounds, rows, wide), lambda j, f: (0, 0, 0, sent(j)))
    return pl.pallas_call(
        feature_kernel,
        out_shape=(out_shape, out),
        grid_spec=pltpu.PrefetchScalarGridSpec(
            num_scalar_prefetch=1, grid=(2 * steps,), in_specs=in_specs, out_specs=(send, own)
        ),
        compiler_params=params(),
        cost_estimate=SHORT,
        name="product" if keys is None else "gate",
    )(flags, *operands)


def filter_kernel(flags, p_own, p_recv, rim, wrapped, f_own, f_recv, rows_ref, v_ref, product, gate):
    rounds, block, lanes = p_own.shape
    size = 2 * block
    side, first = flags[0], flags[1]
    mine = pl.multiple_of(side * block, block)
    other = pl.multiple_of((1 - side) * block, block)
    for r in range(rounds):
        product[r, pl.ds(block + mine, block)] = p_own[r]
        product[r, pl.ds(block + other, block)] = p_recv[r]
        gate[r, pl.ds(mine, block)] = f_own[r]
        gate[r, pl.ds(other, block)] = f_recv[r]

        @pl.when(first == 0)
        def _():
            product[r, 0:block] = rim[r]

        @pl.when(first == 1)
        def _():
            product[r, 0:block] = wrapped[r - 1] if r else jnp.zeros((block, lanes), jnp.bfloat16)

    span = HEAD_DIM * rows_ref.shape[0] // lanes
    width = HEAD_DIM // span
    for tile in range(lanes // HEAD_DIM):
        cut = slice(tile * HEAD_DIM, (tile + 1) * HEAD_DIM)
        windows, gates = [], []
        for r in range(rounds):
            flat = product[r, :, cut].astype(jnp.float32).T.astype(jnp.bfloat16)
            windows += [flat[:, 0:size], flat[:, block : 3 * block]]
            gates.append(gate[r, :, cut].astype(jnp.float32).T)
        for g in range(span):
            row = jnp.broadcast_to(rows_ref[tile * span + g : tile * span + g + 1], (block, size))
            toeplitz = pltpu.roll(row, 0, 1, stride=1, stride_axis=0).astype(jnp.bfloat16)
            here = slice(g * width, (g + 1) * width)
            stacked = jnp.concatenate([w[here] for w in windows], axis=0)
            mixed = lax.dot_general(
                stacked, toeplitz, (((1,), (1,)), ((), ())), preferred_element_type=jnp.float32
            )
            for r in range(rounds):
                for b in range(2):
                    at = (2 * r + b) * width
                    v_ref[r, tile * HEAD_DIM + g * width : tile * HEAD_DIM + (g + 1) * width, b * block : (b + 1) * block] = (
                        gates[r][here, b * block : (b + 1) * block] * mixed[at : at + width]
                    ).astype(jnp.bfloat16)


def filtered_values(
    flags, p_own, p_recv, rim, wrapped, f_own, fk_recv, filter_rows, group, within, channels, total_channels
):
    rounds, block, _ = f_own.shape
    lanes = min(VALUE_LANES, channels)
    steps = channels // lanes
    span = lanes * filter_rows.shape[0] // total_channels
    p_tile = pl.BlockSpec((rounds, block, lanes), lambda j, f: (0, 0, group * steps + j))
    tile = pl.BlockSpec((rounds, block, lanes), lambda j, f: (0, 0, within * steps + j))
    return pl.pallas_call(
        filter_kernel,
        out_shape=jax.ShapeDtypeStruct((rounds, channels, 2 * block), jnp.bfloat16),
        grid_spec=pltpu.PrefetchScalarGridSpec(
            num_scalar_prefetch=1,
            grid=(steps,),
            in_specs=[
                p_tile,
                p_tile,
                p_tile,
                pl.BlockSpec((rounds - 1, block, lanes), lambda j, f: (0, 0, group * steps + j)),
                tile,
                pl.BlockSpec((None, rounds, block, lanes), lambda j, f: (0, 0, 0, within * steps + j)),
                pl.BlockSpec((span, 2 * block), lambda j, f: (group * steps + j, 0)),
            ],
            out_specs=pl.BlockSpec((rounds, lanes, 2 * block), lambda j, f: (0, j, 0)),
            scratch_shapes=[
                pltpu.VMEM((rounds, 3 * block, lanes), jnp.bfloat16),
                pltpu.VMEM((rounds, 2 * block, lanes), jnp.bfloat16),
            ],
        ),
        compiler_params=params(),
        cost_estimate=SHORT,
        name="values",
    )(flags, p_own, p_recv, rim, wrapped, f_own, fk_recv, filter_rows)


PAIR = 2
FLAGS = 3


def gather_rows(side, block, out, own, recv):
    mine = pl.multiple_of(side * block, block)
    other = pl.multiple_of((1 - side) * block, block)
    for r in range(own.shape[0]):
        out[r, pl.ds(mine, block)] = own[r]
        out[r, pl.ds(other, block)] = recv[r]


def attend(jobs, query, key, value, bias, finish):
    def scores_of(job):
        return lax.dot_general(
            key(*job), query(*job), (((1,), (1,)), ((), ())), preferred_element_type=jnp.float32
        )

    following = scores_of(jobs[0])
    for n, job in enumerate(jobs):
        scores = following * (HEAD_DIM**-0.5 * LOG2E) + bias(*job)
        if n + 1 < len(jobs):
            following = scores_of(jobs[n + 1])
        top = jnp.max(scores, axis=0, keepdims=True)
        raised = jnp.exp2(scores - top)
        total = jnp.sum(raised, axis=0, keepdims=True)
        mixed = jnp.dot(value(*job), raised.astype(jnp.bfloat16), preferred_element_type=jnp.float32)
        finish(job, mixed, top, total)


def job_list(rounds, lanes, size):
    return [
        (r, slice(c, c + HEAD_DIM), slice(q, q + HEAD_DIM))
        for r in rounds
        for c in range(0, lanes, HEAD_DIM)
        for q in range(0, size, HEAD_DIM)
    ]


def stat_rows(levels):
    row = lax.broadcasted_iota(jnp.int32, (STAT_ROWS, levels[0].shape[1]), 0)
    table = jnp.zeros(row.shape, jnp.float32)
    for e, level in enumerate(levels):
        high = level.astype(jnp.bfloat16).astype(jnp.float32)
        rest = level - high
        middle = rest.astype(jnp.bfloat16).astype(jnp.float32)
        for k, piece in enumerate((high, middle, rest - middle)):
            table = jnp.where(row == 3 * e + k, piece, table)
    return table.astype(jnp.bfloat16)


def partial_kernel(kinds, flags, start_ref, far_start, q_own, q_recv, wrapped, k_own, k_recv, v_ref, *rest):
    asked = rest[: len(kinds)]
    o_ref = rest[len(kinds)]
    far_o = rest[len(kinds) + 1 : 2 * len(kinds) + 1]
    bias, queries, keys, far_queries = rest[2 * len(kinds) + 1 :]
    rounds, block, lanes = q_own.shape
    size = 2 * block
    last = flags[2]
    key_at = lax.broadcasted_iota(jnp.int32, (size, size), 0)
    for r in range(rounds):
        seen = key_at - size >= start_ref[r]
        if r == 0:
            seen = seen & (last == 0)
        bias[r] = jnp.where(seen, 0.0, MASKED)
    gather_rows(flags[0], block, queries, q_own, q_recv)
    gather_rows(flags[0], block, keys, k_own, k_recv)

    @pl.when(last == 1)
    def _():
        gather_rows(flags[0], block, queries.at[rounds - 1 :], wrapped.at[0:1], wrapped.at[1:2])

    def written(write):
        levels = {}

        def finish(job, mixed, top, total):
            r, cut, span = job
            write(r, cut, span, (mixed * (1.0 / total)).astype(jnp.bfloat16))
            levels[(r, span.start, cut.start)] = top + jnp.log2(total)
            if cut.stop == lanes:
                rows = stat_rows([levels[(r, span.start, c)] for c in range(0, lanes, HEAD_DIM)])
                write(r, slice(lanes, lanes + STAT_ROWS), span, rows)

        return finish

    def put(r, cut, span, value):
        o_ref[r, cut, span] = value

    def source(r):
        return r - last if r else 0

    attend(
        job_list(range(rounds), lanes, size),
        lambda r, cut, span: queries[r, span, cut],
        lambda r, cut, span: keys[source(r), :, cut],
        lambda r, cut, span: v_ref[source(r), cut],
        lambda r, cut, span: bias[r, :, span],
        written(put),
    )
    for n, (reach, key_round, _) in enumerate(kinds):

        @pl.when(flags[FLAGS + n] == 1)
        def _(n=n, reach=reach, key_round=key_round):
            far_queries[pl.ds(pl.multiple_of(flags[0] * block, block), block)] = asked[n][0]
            far_queries[pl.ds(pl.multiple_of((1 - flags[0]) * block, block), block)] = asked[n][1]

            def put(r, cut, span, value):
                far_o[n][cut, span] = value

            attend(
                job_list([key_round], lanes, size),
                lambda r, cut, span: far_queries[span, cut],
                lambda r, cut, span: keys[r, :, cut],
                lambda r, cut, span: v_ref[r, cut],
                lambda r, cut, span: jnp.where(
                    key_at[:, span] - reach * size >= far_start[n, :, span], 0.0, MASKED
                ),
                written(put),
            )


def own_half(group, groups, rounds, block, lanes):
    return pl.BlockSpec((rounds, block, lanes), lambda j, f: (0, 0, f[0] * groups + group))


def partial_attention(
    flags, start, far_start, q_own, q_recv, wrapped, keys, fk_recv, values, asked, kinds, group, groups, within
):
    rounds, block, _ = q_own.shape
    size = 2 * block
    lanes = values.shape[1]
    tile = pl.BlockSpec((rounds, block, lanes), lambda j, f: (0, 0, group))
    rows = lanes + STAT_ROWS
    out = pl.BlockSpec((rows, size), lambda j, f: (0, 0))
    return pl.pallas_call(
        functools.partial(partial_kernel, kinds),
        out_shape=[jax.ShapeDtypeStruct((rounds, rows, size), jnp.bfloat16)]
        + [jax.ShapeDtypeStruct((rows, size), jnp.bfloat16)] * len(kinds),
        grid_spec=pltpu.PrefetchScalarGridSpec(
            num_scalar_prefetch=1,
            grid=(1,),
            in_specs=[
                pl.BlockSpec((rounds, 1, size), lambda j, f: (0, 0, 0)),
                pl.BlockSpec(far_start.shape, lambda j, f: (0, 0, 0)),
                tile,
                tile,
                pl.BlockSpec((2, block, lanes), lambda j, f: (0, 0, group)),
                own_half(group, groups, rounds, block, lanes),
                pl.BlockSpec((None, rounds, block, lanes), lambda j, f: (1, 0, 0, within)),
                pl.BlockSpec((rounds, lanes, size), lambda j, f: (0, 0, 0)),
            ]
            + [pl.BlockSpec((2, block, lanes), lambda j, f: (0, 0, group))] * len(kinds),
            out_specs=[pl.BlockSpec((rounds, rows, size), lambda j, f: (0, 0, 0))] + [out] * len(kinds),
            scratch_shapes=[
                pltpu.VMEM((rounds, size, size), jnp.float32),
                pltpu.VMEM((rounds, size, lanes), jnp.bfloat16),
                pltpu.VMEM((rounds, size, lanes), jnp.bfloat16),
                pltpu.VMEM((size, lanes), jnp.bfloat16),
            ],
        ),
        compiler_params=params(),
        cost_estimate=SHORT,
        name="partial",
    )(flags, start, far_start, q_own, q_recv, wrapped, keys, fk_recv, values, *asked)


def merge_kernel(kinds, flags, start_ref, q_own, q_recv, k_own, k_recv, v_ref, near, *rest):
    far = rest[: len(kinds)]
    own_ref, send_ref, bias, queries, keys, result = rest[len(kinds) :]
    rounds, block, lanes = q_own.shape
    size = 2 * block
    side = flags[0]
    key_at = lax.broadcasted_iota(jnp.int32, (size, size), 0)
    query_at = lax.broadcasted_iota(jnp.int32, (size, size), 1)
    for r in range(rounds):
        bias[r] = jnp.where((key_at >= start_ref[r]) & (key_at <= query_at), 0.0, MASKED)
    gather_rows(side, block, queries, q_own, q_recv)
    gather_rows(side, block, keys, k_own, k_recv)

    def finish(job, mixed, top, total):
        r, cut, span = job
        first = 3 * (cut.start // HEAD_DIM)
        parts, levels = [], []
        for n in range(len(kinds) + 1):
            if n and kinds[n - 1][2] != r:
                continue
            block_of = near[r] if n == 0 else far[n - 1]
            rows = block_of[lanes : lanes + STAT_ROWS, span].astype(jnp.float32)
            level = rows[first : first + 1] + rows[first + 1 : first + 2] + rows[first + 2 : first + 3]
            part = block_of[cut, span].astype(jnp.float32)
            if n:
                asks = flags[FLAGS + len(kinds) + n - 1] == 1
                level, part = jnp.where(asks, level, MASKED), jnp.where(asks, part, 0.0)
            parts.append(part)
            levels.append(level)
        high = functools.reduce(jnp.maximum, levels, top)
        share = jnp.exp2(top - high)
        mixed, total = mixed * share, total * share
        for part, level in zip(parts, levels):
            share = jnp.exp2(level - high)
            mixed, total = mixed + part * share, total + share
        result[r, span, cut] = (mixed * (1.0 / total)).T.astype(jnp.bfloat16)

    attend(
        job_list(range(rounds), lanes, size),
        lambda r, cut, span: queries[r, span, cut],
        lambda r, cut, span: keys[r, :, cut],
        lambda r, cut, span: v_ref[r, cut],
        lambda r, cut, span: bias[r, :, span],
        finish,
    )
    for r in range(rounds):
        own_ref[r] = result[r, pl.ds(pl.multiple_of(side * block, block), block)]
        send_ref[r] = result[r, pl.ds(pl.multiple_of((1 - side) * block, block), block)]


def merged_attention(flags, start, queries, q_recv, keys, fk_recv, values, near, found, place, kinds, group, groups, within):
    rounds, block, _ = q_recv.shape
    size = 2 * block
    lanes = values.shape[1]
    rows = lanes + STAT_ROWS
    own = own_half(group, groups, rounds, block, lanes)
    tile = pl.BlockSpec((rounds, block, lanes), lambda j, f: (0, 0, 0))
    out = jax.ShapeDtypeStruct((rounds, block, lanes), jnp.bfloat16)
    return pl.pallas_call(
        functools.partial(merge_kernel, kinds),
        out_shape=(out, out),
        grid_spec=pltpu.PrefetchScalarGridSpec(
            num_scalar_prefetch=1,
            grid=(1,),
            in_specs=[
                pl.BlockSpec((rounds, 1, size), lambda j, f: (0, 0, 0)),
                own,
                pl.BlockSpec((rounds, block, lanes), lambda j, f: (0, 0, group)),
                own,
                pl.BlockSpec((None, rounds, block, lanes), lambda j, f: (1, 0, 0, within)),
                pl.BlockSpec((rounds, lanes, size), lambda j, f: (0, 0, 0)),
                pl.BlockSpec((rounds, rows, size), lambda j, f: (0, 0, 0)),
            ]
            + [pl.BlockSpec((None, rows, size), lambda j, f: (place, 0, 0))] * len(kinds),
            out_specs=(tile, tile),
            scratch_shapes=[
                pltpu.VMEM((rounds, size, size), jnp.float32),
                pltpu.VMEM((rounds, size, lanes), jnp.bfloat16),
                pltpu.VMEM((rounds, size, lanes), jnp.bfloat16),
                pltpu.VMEM((rounds, size, lanes), jnp.bfloat16),
            ],
        ),
        compiler_params=params(),
        cost_estimate=SHORT,
        name="merged",
    )(flags, start, queries, q_recv, keys, fk_recv, values, near, *found)


def unwritten(shape):
    return pl.pallas_call(
        lambda ref: None,
        out_shape=jax.ShapeDtypeStruct(shape, jnp.bfloat16),
        out_specs=pl.BlockSpec(memory_space=pl.ANY),
        cost_estimate=SHORT,
        name="unwritten",
    )()


def after(value, *others):
    return lax.optimization_barrier((value,) + others)[0]


def body(streams, short_taps, filters, queries, keys, fragment_lengths):
    rounds, block, _, channels = streams.shape
    ctx = lax.axis_size("ctx")
    at = lax.axis_index("ctx")
    side, z = at % 2, at // 2
    depth = ctx // 2
    size = 2 * block
    seq = rounds * ctx * block
    half = channels // 2
    groups = min(GROUPS, half // (PAIR * HEAD_DIM))
    part = half // groups
    halves = min(2, groups)
    per_half = groups // halves

    def moved(value, pairs):
        return lax.ppermute(value, "ctx", pairs)

    swap = [(i, i ^ 1) for i in range(ctx)]

    def ring(d):
        return [(i, (i + 2 * d) % ctx) for i in range(ctx)]

    def along(d, chosen=lambda z: True):
        return [(i, i + 2 * d) for i in range(ctx) if 0 <= i + 2 * d < ctx and chosen(i // 2)]

    def around(d):
        return [(i, (i + 2 * d) % ctx) for i in range(ctx) if not 0 <= i + 2 * d < ctx]

    ends = jnp.cumsum(fragment_lengths)
    begins = ends - fragment_lengths

    def start_at(positions):
        return jnp.max(jnp.where(begins <= positions[..., None], begins, 0), axis=-1)

    def starts_of(superblocks):
        base = superblocks[:, None] * size
        return (start_at(base + jnp.arange(size, dtype=jnp.int32)) - base)[:, None, :]

    def reaches(superblock, d, row=0):
        return start_at(superblock * size + row) < (superblock - d + 1) * size

    far_reach = -(-(seq // 4 - 1) // size)
    kinds, far_pairs, hold, ask, wide, far_starts = [], [], [], [], [], []
    for d in range(2, far_reach + 1):
        for r in range(rounds):
            for color in range(2):
                pairs = along(d, functools.partial(lambda c, s, a: (a // s) % 2 == c, color, d))
                if pairs:
                    kinds.append((d, r, r))
                    far_pairs.append(pairs)
                    theirs, ours = z + d + r * depth, z + r * depth
                    hold.append((z + d < depth) & ((z // d) % 2 == color) & reaches(theirs, d))
                    ask.append((z >= d) & (((z - d) // d) % 2 == color) & reaches(ours, d))
                    wide.append((hold[-1] & reaches(theirs, d, block)) | (ask[-1] & reaches(ours, d, block)))
                    far_starts.append(theirs)
        for r in range(rounds - 1):
            kinds.append((d, r, r + 1))
            far_pairs.append(around(d))
            theirs, ours = z + d + r * depth, z + (r + 1) * depth
            hold.append((z + d >= depth) & reaches(theirs, d))
            ask.append((z < d) & reaches(ours, d))
            wide.append((hold[-1] & reaches(theirs, d, block)) | (ask[-1] & reaches(ours, d, block)))
            far_starts.append(theirs)
    preds = [a | b for a, b in zip(hold, ask)]
    any_far = functools.reduce(jnp.logical_or, preds)
    flags = jnp.stack([side, z == 0, z == depth - 1] + hold + ask).astype(jnp.int32)
    mine = z + jnp.arange(rounds, dtype=jnp.int32) * depth
    own_start = starts_of(mine)
    next_start = starts_of(jnp.where(z == depth - 1, jnp.roll(mine + 1, 1), mine + 1))
    far_start = starts_of(jnp.stack(far_starts))

    tail = streams[:, block - 2 :].transpose(0, 2, 1, 3)
    queries = after(queries, tail)
    tail = moved(tail, [(i, (i + 1) % ctx) for i in range(ctx)])
    q_send = lax.dynamic_slice_in_dim(queries, (1 - side) * half, half, 2)
    q_recv = moved(q_send, swap)
    q_own = lax.dynamic_slice_in_dim(after(queries, q_send), side * half, half, 2)
    n_own = moved(q_own, along(-1))

    tail = jnp.where(at == 0, jnp.concatenate([jnp.zeros_like(tail[:1]), tail[:-1]], axis=0), tail)
    first_layout = streams.transpose(0, 2, 1, 3)
    order = flags
    p_send, p_own = features(order, first_layout, tail, short_taps, None, 0, 1)
    order = after(order, p_send)
    p_recv = moved(p_send, swap)
    q_late = after(q_recv, p_send, n_own)
    n_recv = moved(q_late, along(-1))
    wrapped_send = jnp.stack([q_own[-1], q_late[-1]])
    wrapped = moved(wrapped_send, around(-1))
    gates, fk_recv = [], []
    for h in range(halves):
        if h:
            order = after(order, wrapped_send)
        gates.append(features(order, first_layout, tail, short_taps, keys, h, halves))
        order = after(order, gates[h][0])
        fk_recv.append(moved(gates[h][0], swap))
    rim_send = jnp.where(side == 1, p_own, after(p_recv, order))
    rim = moved(rim_send, along(1))
    rim_wrapped = moved(rim_send[:-1], around(1))

    def chosen_kinds(function, empty, *operands):
        def each(operands):
            return [
                lax.cond(pred, functools.partial(function, n), lambda _: unwritten(empty), operands)
                for n, pred in enumerate(preds)
            ]

        return lax.cond(any_far, each, lambda _: [unwritten(empty) for _ in kinds], operands)

    def fetch(n, operands):
        back = [(b, a) for a, b in far_pairs[n]]

        def whole(operands):
            return moved(jnp.stack([value[kinds[n][2]] for value in operands]), back)

        def front(operands):
            own, recv = (value[kinds[n][2]] for value in operands)
            got = moved(jnp.where(side == 0, own, recv), back)
            return jnp.stack([got, got])

        return lax.cond(wide[n], whole, front, operands)

    asked = chosen_kinds(
        fetch, (2, block, half), *after((q_own, q_late), order, n_recv, wrapped, rim_send)
    )
    order = after(order, asked)

    own_filters = lax.dynamic_slice_in_dim(filters, side * (filters.shape[0] // 2), filters.shape[0] // 2, 0)
    filter_rows = jnp.pad(own_filters[:, ::-1], ((0, 0), (1, 2 * block - 1 - filters.shape[1])))
    out = jnp.zeros((rounds, block, channels), jnp.bfloat16)
    values, near = [], []

    def merge(g, order, out):
        own, send = merged_attention(
            order, own_start, queries, q_recv, keys, fk_recv[g // per_half], values[g], near[g], *far[g], kinds, g, groups,
            g % per_half,
        )
        got = moved(send, swap)
        out = lax.dynamic_update_slice_in_dim(out, own, side * half + g * part, 2)
        out = lax.dynamic_update_slice_in_dim(out, got, (1 - side) * half + g * part, 2)
        return send, out

    def answer(n, operands):
        def whole(pieces):
            return moved(jnp.stack(pieces), far_pairs[n])

        def front(pieces):
            got = moved(jnp.stack([piece[:, :block] for piece in pieces]), far_pairs[n])
            return jnp.pad(got, ((0, 0), (0, 0), (0, size - block)), constant_values=MASKED)

        return lax.cond(wide[n], whole, front, [piece[n] for piece in operands])

    far_pieces = []
    for g in range(groups):
        h, within = g // per_half, g % per_half
        values.append(
            filtered_values(
                order, p_own, p_recv, rim, rim_wrapped, gates[h][1], fk_recv[h], filter_rows,
                g, within, part, half,
            )
        )
        piece, *far_piece = partial_attention(
            order, next_start, far_start, n_own, n_recv, wrapped, keys, fk_recv[h], values[g], asked,
            kinds, g, groups, within,
        )
        order = after(order, piece)
        far_pieces.append(far_piece)
        if g == groups - 1:
            found = chosen_kinds(answer, (groups, part + STAT_ROWS, size), *after(far_pieces, order))
            order = after(order, found)
            piece = after(piece, found)
        near.append(moved(after(piece, *near[-2:-1]), ring(1)))
    far = [(found, g) for g in range(groups)]
    for g in range(groups):
        _, out = merge(g, order, out)
    return out


def solution(mesh):
    placed = (
        P("dp", "ctx", None, "tp"),
        P(None, None, "tp"),
        P("tp", None),
        P("dp", "ctx", "tp"),
        P("dp", "ctx", "tp"),
        P("dp"),
    )
    return jax.shard_map(
        body, mesh=mesh, in_specs=placed, out_specs=P("dp", "ctx", "tp"), check_vma=False
    )
```
